128 devices in a mesh: seq: 32 (over z, x, y_lo), dp: 4 (over y_hi, core).
Axes of the slice: x: 4, y: 4 (y_hi: 2, y_lo: 2; y = y_hi * 2 + y_lo), z: 4, core: 2. Of those that a mesh axis runs over, the one named last changes fastest.
Arguments:
- inputs: bfloat16 [4, 1024, 64, 1024], P('dp', 'seq'), may hold values from -6 to 6
- gate_in: bfloat16 [4, 1024, 64, 1024], P('dp', 'seq'), may hold values from -6 to 6
- cotangent: bfloat16 [4, 1024, 64, 1024], P('dp', 'seq'), may hold values from -6 to 6
- right_factor: bfloat16 [1024, 1024], replicated, may hold values from -0.1875 to 0.1875
- left_factor: bfloat16 [1024, 1024], replicated, may hold values from -0.1875 to 0.1875
- mask_tiles: int32 [8, 8], replicated, may hold values from 0 to 1, as said below
Outputs:
- grad_input: bfloat16 [4, 1024, 64, 1024], P('dp', 'seq')
- grad_gate: bfloat16 [4, 1024, 64, 1024], P('dp', 'seq')
- grad_right: float32 [1024, 1024], P(('seq', 'dp'))
- grad_left: float32 [1024, 1024], P(('seq', 'dp'))
The draws below stay inside these ranges and needn't reach their ends.
Inputs may be any that keep to these rules, and one draw needn't show every extreme that they name: `mask_tiles`: 1 on every diagonal tile, 0 above the diagonal, 0 or 1 below it.
All inputs are finite; a program needn't handle non-finite values.
Results may differ from the reference program's by a relative error of at most 0.0058.
Values may be sent and summed in bfloat16 or wider, within the bound.
No kernel may reach another device: no remote copies, remote signals or barrier semaphores. Data moves between devices by JAX's collectives and lax.ppermute only.
A program may use at most 192 MiB of HBM per device.

```python
import math
import jax
import jax.numpy as jnp
from jax import lax

FAC = 1024
C = 64
TILES = 8
BATCH = 4


def draw_mask_tiles(key, part):
    key = jax.random.fold_in(key, 7)
    coins = jax.random.randint(key, (TILES, TILES), 0, 4)
    below = jnp.tril((coins > 0).astype(jnp.int32), -1)
    return below + jnp.eye(TILES, dtype=jnp.int32)


def level_of(key, shape, pieces, low, top_value):
    def one(axis_at, shards_of):
        heights = jax.random.uniform(jax.random.fold_in(jax.random.fold_in(key, 6), axis_at), (shards_of,), jnp.float32, low / len(pieces), top_value / len(pieces))
        return jnp.repeat(jnp.exp(heights), shape[axis_at] // shards_of).reshape((-1,) + (1,) * (len(shape) - axis_at - 1))

    level = one(*pieces[0])
    for cut in pieces[1:]:
        level = level * one(*cut)
    return level


def normal_values(own_key, extent, width, bound, cuts=(), kind=jnp.bfloat16):
    level = level_of(own_key, extent, cuts, -0.22, 0.18) if cuts else 1.0
    result = jax.random.normal(own_key, extent, jnp.float32) * width * level
    return jnp.minimum(jnp.maximum(result, -bound), bound).astype(kind)


def setup_inputs(seed: int = 0) -> dict:
    streams_of = jax.random.split(jax.random.key(seed), 7)
    inputs = normal_values(streams_of[0], (BATCH, FAC, C, FAC), 1.0, 6.0, ((0, 4), (1, 32)))
    gate_in = normal_values(streams_of[1], (BATCH, FAC, C, FAC), 1.5, 6.0, ((0, 4), (1, 32)))
    cotangent = normal_values(streams_of[2], (BATCH, FAC, C, FAC), 1.0, 6.0, ((0, 4), (1, 32)))
    right_factor = normal_values(streams_of[3], (FAC, FAC), FAC ** -0.5, 0.1875)
    left_factor = normal_values(streams_of[4], (FAC, FAC), FAC ** -0.5, 0.1875)
    mask_tiles = draw_mask_tiles(jax.random.fold_in(streams_of[6], 71), 0)
    return {"inputs": inputs, "gate_in": gate_in, "cotangent": cotangent, "right_factor": right_factor, "left_factor": left_factor, "mask_tiles": mask_tiles}


def expand_mask(mask_tiles, size):
    tiles = mask_tiles.shape[0]
    side = size // tiles
    values = mask_tiles.astype(jnp.float32)
    return jnp.broadcast_to(values[:, None, :, None], (tiles, side, tiles, side)).reshape(size, size)

def reference(inputs, gate_in, cotangent, right_factor, left_factor, mask_tiles):
    full_mask = expand_mask(mask_tiles, FAC)
    right_masked = (right_factor.astype(jnp.float32) * full_mask).astype(jnp.bfloat16).astype(jnp.float32)
    left_masked = (left_factor.astype(jnp.float32) * full_mask).astype(jnp.bfloat16).astype(jnp.float32)

    def one_sequence(operands):
        signal, gate_row, cot_row = operands
        signal_f = signal.astype(jnp.float32)
        first = jnp.einsum('icj,kj->ick', signal_f, right_masked).astype(jnp.bfloat16).astype(jnp.float32)
        mixed = jnp.einsum('ui,ick->uck', left_masked, first).astype(jnp.bfloat16).astype(jnp.float32)
        sig = jax.nn.sigmoid(gate_row.astype(jnp.float32))
        cot_f = cot_row.astype(jnp.float32)
        grad_gate = (cot_f * mixed * sig * (1.0 - sig)).astype(jnp.bfloat16)
        grad_mixed = (cot_f * sig).astype(jnp.bfloat16).astype(jnp.float32)
        grad_first = jnp.einsum('ui,uck->ick', left_masked, grad_mixed).astype(jnp.bfloat16).astype(jnp.float32)
        grad_input = jnp.einsum('ick,kj->icj', grad_first, right_masked).astype(jnp.bfloat16)
        left_term = jnp.einsum('uck,ick->ui', grad_mixed, first)
        right_term = jnp.einsum('ick,icj->kj', grad_first, signal_f)
        return (grad_input, grad_gate, left_term, right_term)
    grad_input, grad_gate, left_terms, right_terms = lax.map(one_sequence, (inputs, gate_in, cotangent))
    scale = 1.0 / math.sqrt(BATCH * C * FAC)
    grad_left = lax.optimization_barrier(jnp.sum(left_terms, axis=0)) * full_mask * scale
    grad_right = lax.optimization_barrier(jnp.sum(right_terms, axis=0)) * full_mask * scale
    return (grad_input, grad_gate, grad_right, grad_left)
```

```python
import math

import jax
import jax.numpy as jnp
from jax import lax
from jax.sharding import PartitionSpec as P

BF = jnp.bfloat16
F32 = jnp.float32


def expand_mask(mask_tiles, size):
    tiles = mask_tiles.shape[0]
    side = size // tiles
    values = mask_tiles.astype(F32)
    return jnp.broadcast_to(values[:, None, :, None], (tiles, side, tiles, side)).reshape(
        size, size
    )


def swap(x):
    return lax.all_to_all(x, "seq", split_axis=0, concat_axis=0, tiled=True)


def shards(inputs, gate_in, cotangent, right_factor, left_factor, mask_tiles):
    width = right_factor.shape[0]
    own_blocks, channels = inputs.shape[1], inputs.shape[2]
    seq_count = lax.axis_size("seq")
    data_count = lax.axis_size("dp")
    per = channels // seq_count
    own_rows = width // (seq_count * data_count)
    seq_at, data_at = lax.axis_index("seq"), lax.axis_index("dp")
    full_mask = expand_mask(mask_tiles, width)
    right_masked = (right_factor.astype(F32) * full_mask).astype(BF)
    left_masked = (left_factor.astype(F32) * full_mask).astype(BF)

    sent = (seq_count, per, own_blocks, width)
    signal = swap(inputs[0].transpose(1, 0, 2).reshape(sent))
    sig = jax.nn.sigmoid(gate_in[0].astype(F32))
    grad_rows = (cotangent[0].astype(F32) * sig).astype(BF)
    grad_rows, signal = lax.optimization_barrier((grad_rows.transpose(1, 0, 2).reshape(sent), signal))
    grad_mixed = swap(grad_rows)

    first = jnp.einsum("qcij,kj->qcik", signal, right_masked, preferred_element_type=F32).astype(BF)
    left_rows = left_masked.reshape(seq_count, own_blocks, seq_count, own_blocks)
    mixed = jnp.einsum("puqi,qcik->pcuk", left_rows, first, preferred_element_type=F32).astype(BF)
    mixed, grad_mixed = lax.optimization_barrier((mixed, grad_mixed))
    mixed_rows = swap(mixed)

    grad_first = jnp.einsum(
        "puqi,pcuk->qcik", left_rows, grad_mixed, preferred_element_type=F32
    ).astype(BF)
    left_term = jnp.einsum("pcuk,qcik->puqi", grad_mixed, first, preferred_element_type=F32)
    right_term = jnp.einsum("qcik,qcij->kj", grad_first, signal, preferred_element_type=F32)
    back = jnp.einsum(
        "qcik,kj->qcij", grad_first, right_masked, preferred_element_type=F32
    ).astype(BF)

    terms = jnp.stack(
        (
            left_term.reshape(seq_count, data_count, own_rows, width),
            right_term.reshape(seq_count, data_count, own_rows, width),
        ),
        2,
    )
    terms = terms.reshape(seq_count, 2, 2, 2, own_rows, width)
    core, high = data_at % 2, data_at // 2
    keep = lax.dynamic_index_in_dim(terms, core, 2, keepdims=False)
    give = lax.dynamic_index_in_dim(terms, 1 - core, 2, keepdims=False)
    flat = [(s, d) for s in range(seq_count) for d in range(data_count)]
    keep = keep + lax.ppermute(give, "dp", [(d, d ^ 1) for d in range(data_count)])
    give = lax.dynamic_index_in_dim(keep, 1 - high, 1, keepdims=False).astype(BF)
    keep = lax.dynamic_index_in_dim(keep, high, 1, keepdims=False)
    pairs = [(s * data_count + d, (s ^ 1) * data_count + (d ^ 2)) for s, d in flat]
    keep = keep + lax.ppermute(give, ("seq", "dp"), pairs).astype(F32)
    keep = keep.astype(BF).reshape(seq_count, 2 * own_rows, width)

    packed = jnp.concatenate((back.reshape(seq_count, per * own_blocks, width), keep), 1)
    packed, mixed_rows = lax.optimization_barrier((packed, mixed_rows))
    packed = swap(packed)

    mixed_rows = mixed_rows.reshape(channels, own_blocks, width).transpose(1, 0, 2)
    sig = jax.nn.sigmoid(gate_in[0].astype(F32))
    cot_f = cotangent[0].astype(F32)
    grad_gate = (cot_f * mixed_rows.astype(F32) * sig * (1.0 - sig)).astype(BF)
    grad_input = packed[:, : per * own_blocks].reshape(channels, own_blocks, width).transpose(1, 0, 2)
    sums = jnp.sum(packed[:, per * own_blocks :].astype(F32), 0)
    owner = (seq_at * data_count + data_at) * own_rows
    scale = 1.0 / math.sqrt(data_count * channels * width)
    mask_rows = lax.dynamic_slice_in_dim(full_mask, owner, own_rows, 0) * scale
    return (
        grad_input[None],
        grad_gate[None],
        sums[own_rows:] * mask_rows,
        sums[:own_rows] * mask_rows,
    )


def solution(mesh):
    placed = (
        P("dp", "seq", None, None),
        P("dp", "seq", None, None),
        P("dp", "seq", None, None),
        P(),
        P(),
        P(),
    )
    return jax.shard_map(
        shards,
        mesh=mesh,
        in_specs=placed,
        out_specs=(
            P("dp", "seq", None, None),
            P("dp", "seq", None, None),
            P(("seq", "dp"), None),
            P(("seq", "dp"), None),
        ),
        check_vma=False,
    )
```

```python
import functools
import math

import jax
import jax.numpy as jnp
from jax import lax
from jax.experimental import pallas as pl
from jax.experimental.pallas import tpu as pltpu
from jax.sharding import PartitionSpec as P

BF = jnp.bfloat16
F32 = jnp.float32
MIB = 1024 * 1024
LANES = 128
OCT = 16
SIDE = 256


def params(mib):
    return pltpu.CompilerParams(vmem_limit_bytes=mib * MIB)


def shape(dims, dtype):
    return jax.ShapeDtypeStruct(dims, dtype)


def dot(a, b, on_a, on_b):
    return lax.dot_general(a, b, (((on_a,), (on_b,)), ((), ())), preferred_element_type=F32)


def to_channels(values, scratch, out_ref):
    rows = values.shape[0]
    for t in range(scratch.shape[0]):
        lanes = slice(t * LANES, (t + 1) * LANES)
        scratch[t] = values[:, :, lanes].reshape(rows * OCT, LANES)
        for c in range(OCT):
            picked = scratch[t, pl.ds(c, rows, stride=OCT), :].astype(BF)
            out_ref[c // 2, c % 2 * rows : (c % 2 + 1) * rows, lanes] = picked


def from_channels(in_ref, scratch):
    rows = in_ref.shape[1] // 2
    for t in range(scratch.shape[0]):
        lanes = slice(t * LANES, (t + 1) * LANES)
        for c in range(OCT):
            picked = in_ref[c // 2, c % 2 * rows : (c % 2 + 1) * rows, lanes].astype(F32)
            scratch[t, pl.ds(c, rows, stride=OCT), :] = picked
        yield lanes, scratch[t].reshape(rows, OCT, LANES)


def spread_kernel(x_ref, out_ref, scratch):
    to_channels(x_ref[0].astype(F32), scratch, out_ref)


def gate_kernel(cot_ref, gate_ref, out_ref, scratch):
    sig = jax.nn.sigmoid(gate_ref[0].astype(F32))
    to_channels(cot_ref[0].astype(F32) * sig, scratch, out_ref)


def gather_kernel(in_ref, out_ref, scratch):
    for lanes, values in from_channels(in_ref, scratch):
        out_ref[0, :, :, lanes] = values.astype(BF)


def gate_back_kernel(in_ref, cot_ref, gate_ref, out_ref, scratch):
    for lanes, mixed in from_channels(in_ref, scratch):
        sig = jax.nn.sigmoid(gate_ref[0, :, :, lanes].astype(F32))
        cot = cot_ref[0, :, :, lanes].astype(F32)
        out_ref[0, :, :, lanes] = (cot * mixed * sig * (1.0 - sig)).astype(BF)


def retile(kernel, out_natural, natural, channeled=None):
    _, rows, channels, width = natural[0].shape
    natural_spec = pl.BlockSpec((1, rows, OCT, width), lambda g: (0, 0, g, 0))
    channel_spec = pl.BlockSpec((OCT // 2, 2 * rows, width), lambda g: (g, 0, 0))
    in_specs = [natural_spec] * len(natural)
    operands = list(natural)
    if channeled is not None:
        in_specs = [channel_spec] + (in_specs if out_natural == 2 else [])
        operands = [channeled] + (operands if out_natural == 2 else [])
    if out_natural:
        out_shape, out_spec = shape(natural[0].shape, BF), natural_spec
    else:
        out_shape, out_spec = shape((channels // 2, 2 * rows, width), BF), channel_spec
    return pl.pallas_call(
        kernel,
        grid=(channels // OCT,),
        in_specs=in_specs,
        out_specs=out_spec,
        out_shape=out_shape,
        scratch_shapes=[pltpu.VMEM((width // LANES, rows * OCT, LANES), F32)],
        compiler_params=params(48),
    )(*operands)


def mask_factor(tiles_ref, in_ref, out_ref):
    count = tiles_ref.shape[0]
    side = in_ref.shape[0] // count
    for a in range(count):
        rows = slice(a * side, (a + 1) * side)
        for b in range(count):
            cols = slice(b * side, (b + 1) * side)
            if b > a:
                out_ref[rows, cols] = jnp.zeros((side, side), BF)
            else:
                value = tiles_ref[a, b].astype(F32)
                out_ref[rows, cols] = (in_ref[rows, cols].astype(F32) * value).astype(BF)


def forward_kernel(tiles_ref, left_ref, right_ref, x_ref, first_ref, mixed_ref, left, right):
    @pl.when(pl.program_id(0) == 0)
    def _():
        mask_factor(tiles_ref, left_ref, left)
        mask_factor(tiles_ref, right_ref, right)

    width = left.shape[0]
    devices, rows = x_ref.shape[0], x_ref.shape[1]
    x = x_ref[...].reshape(width, width)
    for at in range(0, width, SIDE):
        end = at + SIDE
        part = dot(x[:, :end], right[at:end, :end], 1, 1).astype(BF)
        first_ref[:, :, at:end] = part.reshape(devices, rows, SIDE)
    first = first_ref[...].reshape(width, width)
    for at in range(0, width, SIDE):
        end = at + SIDE
        part = dot(left[at:end, :end], first[:end], 1, 0).astype(BF)
        mixed_ref[at // rows : end // rows] = part.reshape(SIDE // rows, rows, width)


def backward_kernel(tiles_ref, left_ref, right_ref, g_ref, first_ref, back_ref, left, right):
    @pl.when(pl.program_id(0) == 0)
    def _():
        mask_factor(tiles_ref, left_ref, left)
        mask_factor(tiles_ref, right_ref, right)

    width = left.shape[0]
    devices, rows = g_ref.shape[0], g_ref.shape[1]
    g = g_ref[...].reshape(width, width)
    for at in range(0, width, SIDE):
        end = at + SIDE
        part = dot(left[at:, at:end], g[at:], 0, 0).astype(BF)
        first_ref[at // rows : end // rows] = part.reshape(SIDE // rows, rows, width)
    first = first_ref[...].reshape(width, width)
    for at in range(0, width, SIDE):
        end = at + SIDE
        part = dot(first[:, at:], right[at:, at:end], 1, 0).astype(BF)
        back_ref[:, :, at:end] = part.reshape(devices, rows, SIDE)


def products(kernel, tiles, left, right, x):
    devices, both, width = x.shape
    rows = both // 2
    part = pl.BlockSpec((devices, rows, width), lambda c: (0, c, 0))
    whole = pl.BlockSpec((width, width), lambda c: (0, 0))
    return pl.pallas_call(
        kernel,
        grid=(2,),
        in_specs=[pl.BlockSpec(memory_space=pltpu.SMEM), whole, whole, part],
        out_specs=(part, part),
        out_shape=(shape(x.shape, BF), shape(x.shape, BF)),
        scratch_shapes=[pltpu.VMEM((width, width), BF), pltpu.VMEM((width, width), BF)],
        compiler_params=params(56),
    )(tiles, left, right, x)


def factor_kernel(core_ref, g_ref, first_ref, gf_ref, x_ref, keep_ref, give_ref, sum_l, sum_r):
    width = sum_l.shape[0]
    step = pl.program_id(0)

    @pl.when(step == 0)
    def _():
        sum_l[...] = jnp.zeros_like(sum_l)
        sum_r[...] = jnp.zeros_like(sum_r)

    g, first = g_ref[...].reshape(width, width), first_ref[...].reshape(width, width)
    gf, x = gf_ref[...].reshape(width, width), x_ref[...].reshape(width, width)
    for at in range(0, width, SIDE):
        end = at + SIDE
        sum_l[at:end, :end] += dot(g[at:end], first[:end], 1, 1)
        sum_r[at:end, :end] += dot(gf[:, at:end], x[:, :end], 0, 0)

    def write(refs):
        for lr, total in enumerate((sum_l, sum_r)):
            own = keep_ref.shape[3]
            split = total[...].reshape(width // (4 * own), 2, 2, own, width)
            for core in range(2):
                refs[core][:, :, lr] = split[:, :, core]

    @pl.when((step == 1) & (core_ref[0] == 0))
    def _():
        write((keep_ref, give_ref))

    @pl.when((step == 1) & (core_ref[0] == 1))
    def _():
        write((give_ref, keep_ref))


def factor_terms(core, g, first, gf, x, own):
    devices, both, width = x.shape
    part = pl.BlockSpec((devices, both // 2, width), lambda c: (0, c, 0))
    dims = (devices, 2, 2, own, width)
    whole = pl.BlockSpec(dims, lambda c: (0, 0, 0, 0, 0))
    return pl.pallas_call(
        factor_kernel,
        grid=(2,),
        in_specs=[pl.BlockSpec(memory_space=pltpu.SMEM)] + [part] * 4,
        out_specs=(whole, whole),
        out_shape=(shape(dims, F32), shape(dims, F32)),
        scratch_shapes=[pltpu.VMEM((width, width), F32), pltpu.VMEM((width, width), F32)],
        compiler_params=params(60),
    )(core, g, first, gf, x)


def add_kernel(high_ref, keep_a, got_a, keep_b, got_b, mine_ref, give_ref):
    mine_ref[...] = (keep_a[:, 0] + got_a[:, 0]).reshape(mine_ref.shape)
    give_ref[...] = (keep_b[:, 0] + got_b[:, 0]).reshape(give_ref.shape).astype(BF)


def add_halves(high, keep, got):
    devices, _, _, own, width = keep.shape
    step = devices // 4

    def half(flip):
        return pl.BlockSpec(
            (step, 1, 2, own, width), lambda g, high: (g, high[0] ^ flip, 0, 0, 0)
        )

    out = pl.BlockSpec((step, 2 * own, width), lambda g, high: (g, 0, 0))
    dims = (devices, 2 * own, width)
    return pl.pallas_call(
        add_kernel,
        grid_spec=pltpu.PrefetchScalarGridSpec(
            num_scalar_prefetch=1,
            grid=(4,),
            in_specs=[half(0), half(0), half(1), half(1)],
            out_specs=(out, out),
        ),
        out_shape=(shape(dims, F32), shape(dims, BF)),
        compiler_params=params(32),
    )(high, keep, got, keep, got)


def swap(x):
    return lax.all_to_all(x, "seq", split_axis=0, concat_axis=0, tiled=True)


def shards(inputs, gate_in, cotangent, right_factor, left_factor, mask_tiles):
    width = right_factor.shape[0]
    rows, channels = inputs.shape[1], inputs.shape[2]
    seq_count = lax.axis_size("seq")
    data_count = lax.axis_size("dp")
    own = width // (seq_count * data_count)
    seq_at, data_at = lax.axis_index("seq"), lax.axis_index("dp")
    core = jnp.full((1,), data_at % 2, jnp.int32)
    high = jnp.full((1,), data_at // 2, jnp.int32)

    signal = swap(retile(spread_kernel, 0, (inputs,)))
    grad_rows = retile(gate_kernel, 0, (cotangent, gate_in))
    grad_rows, signal = lax.optimization_barrier((grad_rows, signal))
    grad_mixed = swap(grad_rows)
    first, mixed = products(forward_kernel, mask_tiles, left_factor, right_factor, signal)
    mixed, grad_mixed = lax.optimization_barrier((mixed, grad_mixed))
    mixed_rows = swap(mixed)
    grad_first, back = products(
        backward_kernel, mask_tiles, left_factor, right_factor, grad_mixed
    )

    keep, give = factor_terms(core, grad_mixed, first, grad_first, signal, own)
    got = lax.ppermute(give, "dp", [(d, d ^ 1) for d in range(data_count)])
    keep, give = add_halves(high, keep, got)
    pairs = [
        (s * data_count + d, (s ^ 1) * data_count + (d ^ 2))
        for s in range(seq_count)
        for d in range(data_count)
    ]
    got = lax.ppermute(give, ("seq", "dp"), pairs)
    keep = (keep + got.astype(F32)).astype(BF)

    packed = jnp.concatenate((back, keep), 1)
    packed, mixed_rows = lax.optimization_barrier((packed, mixed_rows))
    packed = swap(packed)

    grad_gate = retile(gate_back_kernel, 2, (cotangent, gate_in), mixed_rows)
    grad_input = retile(gather_kernel, 1, (inputs,), packed)
    sums = jnp.sum(packed[:, 2 * rows :].astype(F32), 0)
    owner = (seq_at * data_count + data_at) * own
    scale = 1.0 / math.sqrt(data_count * channels * width)
    side = width // mask_tiles.shape[0]
    mask_row = lax.dynamic_slice_in_dim(mask_tiles, owner // side, 1, 0).astype(F32)
    mask_row = jnp.repeat(mask_row, side, axis=1) * scale
    return (grad_input, grad_gate, sums[own:] * mask_row, sums[:own] * mask_row)


def solution(mesh):
    placed = (
        P("dp", "seq", None, None),
        P("dp", "seq", None, None),
        P("dp", "seq", None, None),
        P(),
        P(),
        P(),
    )
    return jax.shard_map(
        shards,
        mesh=mesh,
        in_specs=placed,
        out_specs=(
            P("dp", "seq", None, None),
            P("dp", "seq", None, None),
            P(("seq", "dp"), None),
            P(("seq", "dp"), None),
        ),
        check_vma=False,
    )
```

```python
import math

import jax
import jax.numpy as jnp
from jax import lax
from jax.experimental import pallas as pl
from jax.experimental.pallas import tpu as pltpu
from jax.sharding import PartitionSpec as P

BF = jnp.bfloat16
F32 = jnp.float32
MIB = 1024 * 1024
SUB = 16
SIDE = 256


def params(mib):
    return pltpu.CompilerParams(vmem_limit_bytes=mib * MIB)


def shape(dims, dtype):
    return jax.ShapeDtypeStruct(dims, dtype)


def dot(a, b, on_a, on_b):
    return lax.dot_general(a, b, (((on_a,), (on_b,)), ((), ())), preferred_element_type=F32)


def turn(values):
    size = SUB * SUB
    row = lax.broadcasted_iota(jnp.int32, (size, size), 0)
    col = lax.broadcasted_iota(jnp.int32, (size, size), 1)
    other = row % SUB * SUB + row // SUB
    matrix = jnp.where(col == other, 1.0, 0.0).astype(BF)
    return dot(matrix, values, 1, 0)


def spread_kernel(x_ref, cot_ref, gate_ref, out_ref):
    size, width = SUB * SUB, x_ref.shape[3]
    dims = (SUB // 2, 2, SUB, width)
    out_ref[:, :, 0] = turn(x_ref[0].reshape(size, width)).astype(BF).reshape(dims)
    sig = jax.nn.sigmoid(gate_ref[0].astype(F32))
    grad = (cot_ref[0].astype(F32) * sig).astype(BF)
    out_ref[:, :, 1] = turn(grad.reshape(size, width)).astype(BF).reshape(dims)


def gather_kernel(in_ref, cot_ref, gate_ref, back_ref, grad_ref):
    size, width = SUB * SUB, cot_ref.shape[3]
    dims = (SUB, SUB, width)
    back_ref[0] = turn(in_ref[:, :, 1].reshape(size, width)).astype(BF).reshape(dims)
    mixed = turn(in_ref[:, :, 0].reshape(size, width)).reshape(dims)
    sig = jax.nn.sigmoid(gate_ref[0].astype(F32))
    cot = cot_ref[0].astype(F32)
    grad_ref[0] = (cot * mixed * sig * (1.0 - sig)).astype(BF)


def retile_specs(dims):
    _, rows, channels, width = dims
    natural = pl.BlockSpec((1, SUB, SUB, width), lambda i, c: (0, i, c, 0))
    apart = pl.BlockSpec((SUB // 2, 2, 2, SUB, width), lambda i, c: (c, 0, 0, i, 0))
    return (rows // SUB, channels // SUB), natural, apart


def spread(x, cot, gate):
    _, rows, channels, width = x.shape
    grid, natural, apart = retile_specs(x.shape)
    return pl.pallas_call(
        spread_kernel,
        grid=grid,
        in_specs=[natural] * 3,
        out_specs=apart,
        out_shape=shape((channels // 2, 2, 2, rows, width), BF),
        compiler_params=params(40),
    )(x, cot, gate)


def gather(parts, cot, gate):
    grid, natural, apart = retile_specs(cot.shape)
    return pl.pallas_call(
        gather_kernel,
        grid=grid,
        in_specs=[apart, natural, natural],
        out_specs=(natural, natural),
        out_shape=(shape(cot.shape, BF), shape(cot.shape, BF)),
        compiler_params=params(40),
    )(parts, cot, gate)


def mask_factor(tiles_ref, in_ref, out_ref):
    count = tiles_ref.shape[0]
    side = in_ref.shape[0] // count
    for a in range(count):
        rows = slice(a * side, (a + 1) * side)
        for b in range(count):
            cols = slice(b * side, (b + 1) * side)
            if b > a:
                out_ref[rows, cols] = jnp.zeros((side, side), BF)
            else:
                value = tiles_ref[a, b].astype(F32)
                out_ref[rows, cols] = (in_ref[rows, cols].astype(F32) * value).astype(BF)


def mix_kernel(
    at_ref, tiles_ref, left_ref, right_ref, in_ref,
    out_ref, own_ref, give1_ref, give2_ref, give3_ref,
    left, right, first, grad_first, sum_l, sum_r,
):
    step = pl.program_id(0)

    @pl.when(step == 0)
    def _():
        mask_factor(tiles_ref, left_ref, left)
        mask_factor(tiles_ref, right_ref, right)
        sum_l[...] = jnp.zeros_like(sum_l)
        sum_r[...] = jnp.zeros_like(sum_r)

    width = left.shape[0]
    devices, rows = in_ref.shape[0], in_ref.shape[3]
    blocks = [(at, at + SIDE) for at in range(0, width, SIDE)]
    x = in_ref[:, 0, 0].reshape(width, width)
    g = in_ref[:, 0, 1].reshape(width, width)

    def by_device(part):
        return part.reshape(part.shape[0] // rows, rows, part.shape[1])

    for at, end in blocks:
        first[:, at:end] = dot(x[:, :end], right[at:end, :end], 1, 1).astype(BF)
    for at, end in blocks:
        part = dot(left[at:end, :end], first[:end], 1, 0).astype(BF)
        out_ref[at // rows : end // rows, 0, 0] = by_device(part)
    for at, end in blocks:
        grad_first[at:end] = dot(left[at:, at:end], g[at:], 0, 0).astype(BF)
    for at, end in blocks:
        part = dot(grad_first[:, at:], right[at:, at:end], 1, 0).astype(BF)
        out_ref[:, 0, 1, :, at:end] = by_device(part)

    def add(total, at, end, part):
        inner = total.shape[1:3]
        count = SIDE // (inner[0] * inner[1])
        begin = at // (inner[0] * inner[1])
        total[begin : begin + count, :, :, :end] += part.reshape(count, *inner, end)

    for at, end in blocks:
        add(sum_l, at, end, dot(g[at:end], first[:end], 1, 1))
        add(sum_r, at, end, dot(grad_first[:, at:end], x[:, :end], 0, 0))

    @pl.when(step == 1)
    def _():
        for k, ref in enumerate((own_ref, give1_ref, give2_ref, give3_ref)):
            quarter = at_ref[0] ^ k
            both = (sum_l[:, quarter], sum_r[:, quarter])
            ref[...] = jnp.concatenate(both, axis=1).astype(ref.dtype)


def mix(at, tiles, left, right, parts, own):
    devices, _, _, rows, width = parts.shape
    channel = pl.BlockSpec((devices, 1, 2, rows, width), lambda c: (0, c, 0, 0, 0))
    factor = pl.BlockSpec((width, width), lambda c: (0, 0), pipeline_mode=pl.Buffered(1))
    quarter = pl.BlockSpec((devices, 2 * own, width), lambda c: (0, 0, 0))
    smem = pl.BlockSpec(memory_space=pltpu.SMEM)
    square = pltpu.VMEM((width, width), BF)
    total = pltpu.VMEM((devices, rows // own, own, width), F32)
    dims = (devices, 2 * own, width)
    return pl.pallas_call(
        mix_kernel,
        grid=(2,),
        in_specs=[smem, smem, factor, factor, channel],
        out_specs=(channel,) + (quarter,) * 4,
        out_shape=(shape(parts.shape, BF), shape(dims, F32)) + (shape(dims, BF),) * 3,
        scratch_shapes=[square, square, square, square, total, total],
        compiler_params=params(62),
    )(at, tiles, left, right, parts)


def swap(x):
    return lax.all_to_all(x, "seq", split_axis=0, concat_axis=0, tiled=True)


def shards(inputs, gate_in, cotangent, right_factor, left_factor, mask_tiles):
    width = right_factor.shape[0]
    channels = inputs.shape[2]
    seq_count = lax.axis_size("seq")
    data_count = lax.axis_size("dp")
    own = width // (seq_count * data_count)
    seq_at, data_at = lax.axis_index("seq"), lax.axis_index("dp")

    parts = swap(spread(inputs, cotangent, gate_in))
    at = jnp.full((1,), data_at, jnp.int32)
    parts, total, *give = mix(at, mask_tiles, left_factor, right_factor, parts, own)

    got = []
    for k in range(1, data_count):
        pairs = [
            (s * data_count + d, (s ^ (k // 2)) * data_count + (d ^ k))
            for s in range(seq_count)
            for d in range(data_count)
        ]
        got.append(lax.ppermute(give[k - 1], ("seq", "dp"), pairs))
    parts = swap(parts)
    total, parts = lax.optimization_barrier((total, parts))
    for other in got:
        total = total + other.astype(F32)
    total = swap(total.astype(BF))
    grad_input, grad_gate = gather(parts, cotangent, gate_in)

    sums = jnp.sum(total.astype(F32), 0)
    owner = (seq_at * data_count + data_at) * own
    scale = 1.0 / math.sqrt(data_count * channels * width)
    side = width // mask_tiles.shape[0]
    mask_row = lax.dynamic_slice_in_dim(mask_tiles, owner // side, 1, 0).astype(F32)
    mask_row = jnp.repeat(mask_row, side, axis=1) * scale
    return (grad_input, grad_gate, sums[own:] * mask_row, sums[:own] * mask_row)


def solution(mesh):
    placed = (
        P("dp", "seq", None, None),
        P("dp", "seq", None, None),
        P("dp", "seq", None, None),
        P(),
        P(),
        P(),
    )
    return jax.shard_map(
        shards,
        mesh=mesh,
        in_specs=placed,
        out_specs=(
            P("dp", "seq", None, None),
            P("dp", "seq", None, None),
            P(("seq", "dp"), None),
            P(("seq", "dp"), None),
        ),
        check_vma=False,
    )
```

```python
import math

import jax
import jax.numpy as jnp
from jax import lax
from jax.experimental import pallas as pl
from jax.experimental.pallas import tpu as pltpu
from jax.sharding import PartitionSpec as P

BF = jnp.bfloat16
F32 = jnp.float32
MIB = 1024 * 1024
SUB = 16
SIDE = 256


def params(mib):
    return pltpu.CompilerParams(vmem_limit_bytes=mib * MIB)


def shape(dims, dtype):
    return jax.ShapeDtypeStruct(dims, dtype)


def in_hbm(x):
    return pltpu.with_memory_space_constraint(x, pltpu.HBM)


def dot(a, b, on_a, on_b):
    return lax.dot_general(a, b, (((on_a,), (on_b,)), ((), ())), preferred_element_type=F32)


def turn(values):
    size = SUB * SUB
    row = lax.broadcasted_iota(jnp.int32, (size, size), 0)
    col = lax.broadcasted_iota(jnp.int32, (size, size), 1)
    other = row % SUB * SUB + row // SUB
    matrix = jnp.where(col == other, 1.0, 0.0).astype(BF)
    return dot(matrix, values, 1, 0)


def spread_kernel(place_ref, x_ref, cot_ref, gate_ref, out_ref, place_out_ref):
    for k in range(place_ref.shape[0]):
        place_out_ref[k] = place_ref[k]
    size, width = SUB * SUB, x_ref.shape[3]
    dims = (SUB // 2, 2, SUB, width)
    out_ref[:, :, 0] = turn(x_ref[0].reshape(size, width)).astype(BF).reshape(dims)
    sig = jax.nn.sigmoid(gate_ref[0].astype(F32))
    grad = (cot_ref[0].astype(F32) * sig).astype(BF)
    out_ref[:, :, 1] = turn(grad.reshape(size, width)).astype(BF).reshape(dims)


def gather_kernel(in_ref, cot_ref, gate_ref, back_ref, grad_ref):
    size, width = SUB * SUB, cot_ref.shape[3]
    dims = (SUB, SUB, width)
    back_ref[0] = turn(in_ref[:, :, 1].reshape(size, width)).astype(BF).reshape(dims)
    mixed = turn(in_ref[:, :, 0].reshape(size, width)).reshape(dims)
    sig = jax.nn.sigmoid(gate_ref[0].astype(F32))
    cot = cot_ref[0].astype(F32)
    grad_ref[0] = (cot * mixed * sig * (1.0 - sig)).astype(BF)


def retile_specs(dims):
    _, rows, channels, width = dims
    natural = pl.BlockSpec((1, SUB, SUB, width), lambda i, c: (0, i, c, 0))
    apart = pl.BlockSpec((SUB // 2, 2, 2, SUB, width), lambda i, c: (c, 0, 0, i, 0))
    return (rows // SUB, channels // SUB), natural, apart


def spread(place, x, cot, gate):
    _, rows, channels, width = x.shape
    grid, natural, apart = retile_specs(x.shape)
    smem = pl.BlockSpec(memory_space=pltpu.SMEM)
    return pl.pallas_call(
        spread_kernel,
        grid=grid,
        in_specs=[smem] + [natural] * 3,
        out_specs=(apart, smem),
        out_shape=(
            pltpu.HBM((channels // 2, 2, 2, rows, width), BF),
            shape(place.shape, place.dtype),
        ),
        compiler_params=params(40),
    )(place, in_hbm(x), in_hbm(cot), in_hbm(gate))


def gather(parts, cot, gate):
    grid, natural, apart = retile_specs(cot.shape)
    return pl.pallas_call(
        gather_kernel,
        grid=grid,
        in_specs=[apart, natural, natural],
        out_specs=(natural, natural),
        out_shape=(pltpu.HBM(cot.shape, BF), pltpu.HBM(cot.shape, BF)),
        compiler_params=params(40),
    )(in_hbm(parts), in_hbm(cot), in_hbm(gate))


def mask_factor(tiles_ref, in_ref, out_ref):
    count = tiles_ref.shape[0]
    side = in_ref.shape[0] // count
    for a in range(count):
        rows = slice(a * side, (a + 1) * side)
        for b in range(count):
            cols = slice(b * side, (b + 1) * side)
            if b > a:
                out_ref[rows, cols] = jnp.zeros((side, side), BF)
            else:
                value = tiles_ref[a, b].astype(F32)
                out_ref[rows, cols] = (in_ref[rows, cols].astype(F32) * value).astype(BF)


def by_device(part, rows):
    return part.reshape(part.shape[0] // rows, rows, part.shape[1])


def mix_kernel(
    place_ref, tiles_ref, left_ref, right_ref, in_ref,
    out_ref, grad_ref, right_out_ref, keep_ref, give_ref,
    left, left_t, right, first, sum_l, sum_r,
):
    step = pl.program_id(0)

    @pl.when(step == 0)
    def _():
        mask_factor(tiles_ref, left_ref, left)
        mask_factor(tiles_ref, right_ref, right)
        left_t[...] = left[...].T
        right_out_ref[...] = right[...]
        sum_l[...] = jnp.zeros_like(sum_l)
        sum_r[...] = jnp.zeros_like(sum_r)

    width = left.shape[0]
    rows = in_ref.shape[3]
    blocks = [(at, at + SIDE) for at in range(0, width, SIDE)]
    x = in_ref[:, 0, 0].reshape(width, width)
    g = in_ref[:, 0, 1].reshape(width, width)
    for at, end in blocks:
        first[:, at:end] = dot(x[:, :end], right[at:end, :end], 1, 1).astype(BF)
    for at, end in blocks:
        part = dot(left[at:end, :end], first[:end], 1, 0).astype(BF)
        out_ref[at // rows : end // rows, 0, 0] = by_device(part, rows)
    for at, end in blocks:
        part = dot(left_t[at:end, at:], g[at:], 1, 0).astype(BF)
        grad_ref[at // rows : end // rows, 0] = by_device(part, rows)
    grad_first = grad_ref[...].reshape(width, width)

    def add(total, at, end, part):
        _, inner, own, _ = total.shape
        count = SIDE // (inner * own)
        begin = at // (inner * own)
        total[begin : begin + count, :, :, :end] += part.reshape(count, inner, own, end)

    for at, end in blocks:
        add(sum_l, at, end, dot(g[at:end], first[:end], 1, 1))
        add(sum_r, at, end, dot(grad_first[:, at:end], x[:, :end], 0, 0))

    @pl.when(step == 1)
    def _():
        core = place_ref[0] % 2
        for ref, part in ((keep_ref, core), (give_ref, 1 - core)):
            both = (sum_l[:, part], sum_r[:, part])
            ref[...] = jnp.concatenate(both, axis=1).astype(ref.dtype)


def mix(place, tiles, left, right, parts, own):
    devices, _, _, rows, width = parts.shape
    groups = width // (2 * own)
    channel = pl.BlockSpec((devices, 1, 2, rows, width), lambda c: (0, c, 0, 0, 0))
    mixed = pl.BlockSpec((devices, 1, 1, rows, width), lambda c: (0, c, 0, 0, 0))
    grad = pl.BlockSpec((devices, 1, rows, width), lambda c: (0, c, 0, 0))
    factor = pl.BlockSpec((width, width), lambda c: (0, 0))
    half = pl.BlockSpec((groups, 2 * own, width), lambda c: (0, 0, 0))
    smem = pl.BlockSpec(memory_space=pltpu.SMEM)
    square = pltpu.VMEM((width, width), BF)
    total = pltpu.VMEM((groups, 2, own, width), F32)
    dims = (groups, 2 * own, width)
    return pl.pallas_call(
        mix_kernel,
        grid=(2,),
        in_specs=[smem, smem, factor, factor, channel],
        out_specs=(mixed, grad, factor, half, half),
        out_shape=(
            pltpu.HBM(parts.shape, BF),
            pltpu.HBM((devices, 2, rows, width), BF),
            pltpu.HBM((width, width), BF),
            pltpu.HBM(dims, F32),
            pltpu.HBM(dims, BF),
        ),
        scratch_shapes=[square, square, square, square, total, total],
        compiler_params=params(62),
    )(place, tiles, in_hbm(left), in_hbm(right), in_hbm(parts))


def back_kernel(right_ref, grad_ref, parts_ref, out_ref):
    width = right_ref.shape[0]
    rows = grad_ref.shape[2]
    grad_first = grad_ref[...].reshape(width, width)
    for at in range(0, width, SIDE):
        end = at + SIDE
        part = dot(grad_first[:, at:], right_ref[at:, at:end], 1, 0).astype(BF)
        out_ref[:, 0, 0, :, at:end] = by_device(part, rows)


def back(right, grad_first, parts):
    devices, _, _, rows, width = parts.shape
    return pl.pallas_call(
        back_kernel,
        grid=(2,),
        in_specs=[
            pl.BlockSpec((width, width), lambda c: (0, 0)),
            pl.BlockSpec((devices, 1, rows, width), lambda c: (0, c, 0, 0)),
            pl.BlockSpec(memory_space=pl.ANY),
        ],
        out_specs=pl.BlockSpec((devices, 1, 1, rows, width), lambda c: (0, c, 1, 0, 0)),
        out_shape=pltpu.HBM(parts.shape, BF),
        input_output_aliases={2: 0},
        compiler_params=params(40),
    )(in_hbm(right), in_hbm(grad_first), in_hbm(parts))


def add_kernel(keep_ref, got_ref, parts_ref, sum_ref, parts_out_ref):
    sum_ref[...] = (keep_ref[...] + got_ref[...].astype(F32)).astype(BF)


def add(keep, got, parts):
    groups, rows, width = keep.shape
    step = groups // 4
    block = pl.BlockSpec((step, rows, width), lambda g: (g, 0, 0))
    whole = pl.BlockSpec(memory_space=pl.ANY)
    return pl.pallas_call(
        add_kernel,
        grid=(4,),
        in_specs=[block, block, whole],
        out_specs=(block, whole),
        out_shape=(pltpu.HBM(keep.shape, BF), pltpu.HBM(parts.shape, BF)),
        input_output_aliases={2: 1},
        compiler_params=params(16),
    )(in_hbm(keep), in_hbm(got), in_hbm(parts))


def tie_kernel(total_ref, parts_ref, out_ref):
    pass


def tie(total, parts):
    whole = pl.BlockSpec(memory_space=pl.ANY)
    return pl.pallas_call(
        tie_kernel,
        in_specs=[whole, whole],
        out_specs=whole,
        out_shape=pltpu.HBM(total.shape, BF),
        input_output_aliases={0: 0},
    )(in_hbm(total), in_hbm(parts))


def finish_kernel(count, scale, place_ref, tiles_ref, in_ref, left_ref, right_ref):
    own, width = left_ref.shape
    side = width // tiles_ref.shape[0]
    row = (place_ref[1] * count + place_ref[0]) * own // side
    sums = jnp.sum(in_ref[...].astype(F32), 0)
    for tile in range(tiles_ref.shape[0]):
        lanes = slice(tile * side, (tile + 1) * side)
        factor = tiles_ref[row, tile].astype(F32) * scale
        left_ref[:, lanes] = sums[:own, lanes] * factor
        right_ref[:, lanes] = sums[own:, lanes] * factor


def finish(place, tiles, total, count, scale):
    _, both, width = total.shape
    smem = pl.BlockSpec(memory_space=pltpu.SMEM)
    vmem = pl.BlockSpec(memory_space=pltpu.VMEM)
    out = shape((both // 2, width), F32)
    return pl.pallas_call(
        lambda *refs: finish_kernel(count, scale, *refs),
        in_specs=[smem, smem, vmem],
        out_specs=(vmem, vmem),
        out_shape=(out, out),
        compiler_params=params(16),
    )(place, tiles, total)


def swap(x):
    return lax.all_to_all(x, "seq", split_axis=0, concat_axis=0, tiled=True)


def shards(inputs, gate_in, cotangent, right_factor, left_factor, mask_tiles):
    width = right_factor.shape[0]
    channels = inputs.shape[2]
    seq_count = lax.axis_size("seq")
    data_count = lax.axis_size("dp")
    own = width // (seq_count * data_count)
    place = jnp.stack((lax.axis_index("dp"), lax.axis_index("seq"))).astype(jnp.int32)

    parts, place = spread(place, inputs, cotangent, gate_in)
    parts = swap(parts)
    mixed, grad_first, right, keep, give = mix(
        place, mask_tiles, left_factor, right_factor, parts, own
    )
    got = lax.ppermute(give, "dp", [(d, d ^ 1) for d in range(data_count)])
    parts = back(right, grad_first, mixed)
    total, parts = add(keep, got, parts)
    parts = swap(parts)
    total = tie(total, parts)
    same_core = [
        [s * data_count + d for s in range(seq_count) for d in range(core, data_count, 2)]
        for core in range(2)
    ]
    total = lax.all_to_all(
        total,
        ("seq", "dp"),
        split_axis=0,
        concat_axis=0,
        tiled=True,
        axis_index_groups=same_core,
    )
    grad_input, grad_gate = gather(parts, cotangent, gate_in)
    scale = 1.0 / math.sqrt(data_count * channels * width)
    grad_left, grad_right = finish(place, mask_tiles, total, data_count, scale)
    return grad_input, grad_gate, grad_right, grad_left


def solution(mesh):
    placed = (
        P("dp", "seq", None, None),
        P("dp", "seq", None, None),
        P("dp", "seq", None, None),
        P(),
        P(),
        P(),
    )
    return jax.shard_map(
        shards,
        mesh=mesh,
        in_specs=placed,
        out_specs=(
            P("dp", "seq", None, None),
            P("dp", "seq", None, None),
            P(("seq", "dp"), None),
            P(("seq", "dp"), None),
        ),
        check_vma=False,
    )
```

```python
import math

import jax
import jax.numpy as jnp
from jax import lax
from jax.experimental import pallas as pl
from jax.experimental.pallas import tpu as pltpu
from jax.sharding import PartitionSpec as P

BF = jnp.bfloat16
F32 = jnp.float32
MIB = 1024 * 1024
LANES = 128
SUB = 16
SIDE = 256


def params(mib):
    return pltpu.CompilerParams(vmem_limit_bytes=mib * MIB)


def shape(dims, dtype):
    return jax.ShapeDtypeStruct(dims, dtype)


def in_hbm(x):
    return pltpu.with_memory_space_constraint(x, pltpu.HBM)


def dot(a, b, on_a, on_b):
    return lax.dot_general(a, b, (((on_a,), (on_b,)), ((), ())), preferred_element_type=F32)


def turn(values):
    size = SUB * SUB
    row = lax.broadcasted_iota(jnp.int32, (size, size), 0)
    col = lax.broadcasted_iota(jnp.int32, (size, size), 1)
    other = row % SUB * SUB + row // SUB
    matrix = jnp.where(col == other, 1.0, 0.0).astype(BF)
    return dot(matrix, values, 1, 0)


def spread_kernel(place_ref, x_ref, cot_ref, gate_ref, out_ref, place_out_ref):
    for k in range(place_ref.shape[0]):
        place_out_ref[k] = place_ref[k]
    size, width = SUB * SUB, x_ref.shape[3]
    dims = (SUB // 2, 2, SUB, width)
    for at in range(0, x_ref.shape[1], SUB):
        rows = slice(at, at + SUB)
        part = turn(x_ref[0, rows].reshape(size, width))
        out_ref[:, :, 0, rows] = part.astype(BF).reshape(dims)
        tanh = jnp.tanh(gate_ref[0, rows].astype(F32) * 0.5)
        grad = (cot_ref[0, rows].astype(F32) * (0.5 + 0.5 * tanh)).astype(BF)
        part = turn(grad.reshape(size, width))
        out_ref[:, :, 1, rows] = part.astype(BF).reshape(dims)


def spread(place, x, cot, gate):
    _, rows, channels, width = x.shape
    natural = pl.BlockSpec((1, rows, SUB, width), lambda c: (0, 0, c, 0))
    smem = pl.BlockSpec(memory_space=pltpu.SMEM)
    return pl.pallas_call(
        spread_kernel,
        grid=(channels // SUB,),
        in_specs=[smem] + [natural] * 3,
        out_specs=(
            pl.BlockSpec((SUB // 2, 2, 2, rows, width), lambda c: (c, 0, 0, 0, 0)),
            smem,
        ),
        out_shape=(
            pltpu.HBM((channels // 2, 2, 2, rows, width), BF),
            shape(place.shape, place.dtype),
        ),
        compiler_params=params(48),
    )(place, in_hbm(x), in_hbm(cot), in_hbm(gate))


def gather_kernel(in_ref, cot_ref, gate_ref, after_ref, back_ref, grad_ref):
    size, width = SUB * SUB, cot_ref.shape[3]
    dims = (SUB, SUB, width)
    tiles = width // LANES
    halves = cot_ref.shape[1] // SUB

    def rows_of(array, half):
        columns = []
        for tile in range(tiles):
            at = [((c * 2 + array) * tiles + tile) * halves + half for c in range(2)]
            both = jnp.stack((in_ref[:, at[0]], in_ref[:, at[1]]), 1)
            columns.append(both.reshape(size, LANES))
        return turn(jnp.concatenate(columns, 1))

    for half in range(halves):
        rows = slice(half * SUB, (half + 1) * SUB)
        back_ref[0, rows] = rows_of(1, half).astype(BF).reshape(dims)
        mixed = rows_of(0, half).reshape(dims)
        tanh = jnp.tanh(gate_ref[0, rows].astype(F32) * 0.5)
        slope = 0.25 * (1.0 - tanh) * (1.0 + tanh)
        grad_ref[0, rows] = (cot_ref[0, rows].astype(F32) * mixed * slope).astype(BF)


def gather(parts, cot, gate, after):
    _, rows, channels, width = cot.shape
    natural = pl.BlockSpec((1, rows, SUB, width), lambda c: (0, 0, c, 0))
    blocks = 4 * rows * width // (SUB * LANES)
    return pl.pallas_call(
        gather_kernel,
        grid=(channels // SUB,),
        in_specs=[
            pl.BlockSpec((SUB // 2, blocks, SUB, LANES), lambda c: (c, 0, 0, 0)),
            natural,
            natural,
            pl.BlockSpec(memory_space=pl.ANY),
        ],
        out_specs=(natural, natural),
        out_shape=(pltpu.HBM(cot.shape, BF), pltpu.HBM(cot.shape, BF)),
        compiler_params=params(48),
    )(in_hbm(parts), in_hbm(cot), in_hbm(gate), after)


def mask_factor(tiles_ref, ref):
    count = tiles_ref.shape[0]
    side = ref.shape[0] // count
    for a in range(count):
        rows = slice(a * side, (a + 1) * side)
        for b in range(count):
            cols = slice(b * side, (b + 1) * side)
            if b > a:
                ref[rows, cols] = jnp.zeros((side, side), BF)
            else:
                value = tiles_ref[a, b].astype(F32)
                ref[rows, cols] = (ref[rows, cols].astype(F32) * value).astype(BF)


def put_tiles(ref, lead, part, rows):
    devices, halves = part.shape[0] // rows, rows // SUB
    for tile in range(part.shape[1] // LANES):
        piece = part[:, tile * LANES : (tile + 1) * LANES]
        at = tile * halves
        ref[lead : lead + devices, at : at + halves] = piece.reshape(devices, halves, SUB, LANES)


def mix_kernel(
    place_ref, tiles_ref, left_hbm, right_hbm, in_hbm_ref,
    out_hbm, grad_hbm, right_out_hbm, keep_hbm, give_hbm,
    left, right, xs, gs, first, grad, mixed, total, keep, give, in_sems, out_sems,
):
    width = left.shape[0]
    rows = xs.shape[2]
    devices = width // rows
    blocks = [(at, at + SIDE) for at in range(0, width, SIDE)]

    loads = [
        pltpu.make_async_copy(src, dst, in_sems.at[k])
        for k, (src, dst) in enumerate(
            (
                (right_hbm, right),
                (in_hbm_ref.at[:, 0, 0], xs.at[0]),
                (in_hbm_ref.at[:, 1, 0], xs.at[1]),
                (left_hbm, left),
                (in_hbm_ref.at[:, 0, 1], gs.at[0]),
                (in_hbm_ref.at[:, 1, 1], gs.at[1]),
            )
        )
    ]
    for load in loads:
        load.start()
    stores = []

    def store(src, dst):
        copy = pltpu.make_async_copy(src, dst, out_sems.at[len(stores)])
        copy.start()
        stores.append(copy)

    loads[0].wait()
    mask_factor(tiles_ref, right)
    store(right, right_out_hbm)
    for c in range(2):
        loads[1 + c].wait()
        x = xs[c].reshape(width, width)
        for at, end in blocks:
            first[c, :, at:end] = dot(x[:, :end], right[at:end, :end], 1, 1).astype(BF)
    loads[3].wait()
    mask_factor(tiles_ref, left)
    for c in range(2):
        loads[4 + c].wait()
        g = gs[c].reshape(width, width)
        for at, end in blocks:
            grad[c, at:end] = dot(left[at:, at:end], g[at:], 0, 0).astype(BF)
        store(grad.at[c], grad_hbm.at[c])

    core = place_ref[0] % 2
    side = width // tiles_ref.shape[0]
    per_tile = devices * side // width
    for at, end in blocks:
        sums = [None, None]
        for c in range(2):
            x, g = xs[c].reshape(width, width), gs[c].reshape(width, width)
            left_part = dot(g[at:end], first[c, :end], 1, 1)
            right_part = dot(grad[c, :, at:end], x[:, :end], 0, 0)
            for k, part in enumerate((left_part, right_part)):
                sums[k] = part if sums[k] is None else sums[k] + part
        for k in range(2):
            total[k, :, :, :, :, :end] = sums[k].reshape(total.shape[1:5] + (end,))
        for s in range(at // rows, end // rows):
            lower = s < devices // 2
            mirror = devices - 1 - s
            first_tile = 0 if lower else (mirror // per_tile) + 1
            for k in range(2):
                to = (s if lower else mirror) if k == 0 else (mirror if lower else s)
                for tile in range(s // per_tile + 1):
                    cols = slice(tile * LANES, (tile + 1) * LANES)
                    place = first_tile + tile
                    own = total[k, s - at // rows, :, core, :, cols]
                    keep[to, place] = own.reshape(SUB, LANES)
                    other = total[k, s - at // rows, :, 1 - core, :, cols]
                    give[to, place] = other.reshape(SUB, LANES).astype(BF)
    store(keep, keep_hbm)
    store(give, give_hbm)

    count = mixed.shape[2]
    for c in range(2):
        for at, end in blocks:
            part = dot(left[at:end, :end], first[c, :end], 1, 0).astype(BF)
            put_tiles(mixed.at[c], at // rows, part, rows)
        store(mixed.at[c], out_hbm.at[:, pl.ds(2 * c * count, count)])
    for copy in stores:
        copy.wait()


def mix(place, tiles, left, right, parts, own):
    devices, _, _, rows, width = parts.shape
    halves = rows // SUB
    count = width // LANES * halves
    terms = tiles.shape[0] + 1
    smem = pl.BlockSpec(memory_space=pltpu.SMEM)
    whole = pl.BlockSpec(memory_space=pl.ANY)
    square = pltpu.VMEM((width, width), BF)
    channels = pltpu.VMEM((2, devices, rows, width), BF)
    squares = pltpu.VMEM((2, width, width), BF)
    dims = (devices, terms, SUB, LANES)
    return pl.pallas_call(
        mix_kernel,
        in_specs=[smem, smem, whole, whole, whole],
        out_specs=(whole,) * 5,
        out_shape=(
            pltpu.HBM((devices, 4 * count + terms, SUB, LANES), BF),
            pltpu.HBM((2, width, width), BF),
            pltpu.HBM((width, width), BF),
            pltpu.HBM(dims, F32),
            pltpu.HBM(dims, BF),
        ),
        scratch_shapes=[
            square,
            square,
            channels,
            channels,
            squares,
            squares,
            pltpu.VMEM((2, devices, count, SUB, LANES), BF),
            pltpu.VMEM((2, SIDE // rows, halves, 2, own, width), F32),
            pltpu.VMEM(dims, F32),
            pltpu.VMEM(dims, BF),
            pltpu.SemaphoreType.DMA((6,)),
            pltpu.SemaphoreType.DMA((7,)),
        ],
        compiler_params=params(56),
    )(place, tiles, in_hbm(left), in_hbm(right), in_hbm(parts))


def back_kernel(rows, right_ref, grad_ref, parts_ref, out_ref):
    width = right_ref.shape[0]
    for at in range(0, width, SIDE):
        end = at + SIDE
        part = dot(grad_ref[0, :, at:], right_ref[at:, at:end], 1, 0).astype(BF)
        halves = rows // SUB
        for tile in range(SIDE // LANES):
            piece = part[:, tile * LANES : (tile + 1) * LANES]
            place = (at // LANES + tile) * halves
            out_ref[:, place : place + halves] = piece.reshape(-1, halves, SUB, LANES)


def back(right, grad_first, parts, rows):
    _, width, _ = grad_first.shape
    devices = parts.shape[0]
    count = width // LANES * (rows // SUB)
    return pl.pallas_call(
        lambda *refs: back_kernel(rows, *refs),
        grid=(2,),
        in_specs=[
            pl.BlockSpec((width, width), lambda c: (0, 0)),
            pl.BlockSpec((1, width, width), lambda c: (c, 0, 0)),
            pl.BlockSpec(memory_space=pl.ANY),
        ],
        out_specs=pl.BlockSpec((devices, count, SUB, LANES), lambda c: (0, 2 * c + 1, 0, 0)),
        out_shape=pltpu.HBM(parts.shape, BF),
        input_output_aliases={2: 0},
        compiler_params=params(40),
    )(in_hbm(right), in_hbm(grad_first), in_hbm(parts))


def add_kernel(keep_ref, got_ref, parts_ref, out_ref, total, sem):
    total[...] = (keep_ref[...] + got_ref[...].astype(F32)).astype(BF)
    terms = total.shape[1]
    copy = pltpu.make_async_copy(
        total, out_ref.at[:, pl.ds(out_ref.shape[1] - terms, terms)], sem
    )
    copy.start()
    copy.wait()


def add(keep, got, parts):
    vmem = pl.BlockSpec(memory_space=pltpu.VMEM)
    whole = pl.BlockSpec(memory_space=pl.ANY)
    return pl.pallas_call(
        add_kernel,
        in_specs=[vmem, vmem, whole],
        out_specs=whole,
        out_shape=pltpu.HBM(parts.shape, BF),
        input_output_aliases={2: 0},
        scratch_shapes=[pltpu.VMEM(keep.shape, BF), pltpu.SemaphoreType.DMA],
        compiler_params=params(16),
    )(keep, got, in_hbm(parts))


def fold_kernel(place_ref, parts_ref, mine_ref, other_ref, got, total, sem):
    terms, own = mine_ref.shape[0], mine_ref.shape[1]
    copy = pltpu.make_async_copy(
        parts_ref.at[:, pl.ds(parts_ref.shape[1] - terms, terms)], got, sem
    )
    copy.start()
    copy.wait()
    total[...] = jnp.sum(got[...].astype(F32), 0).reshape(terms, 2, own, LANES)
    high = place_ref[0] // 2
    mine_ref[...] = total[:, high]
    other_ref[...] = total[:, 1 - high]


def fold(place, parts, terms, own):
    vmem = pl.BlockSpec(memory_space=pltpu.VMEM)
    out = shape((terms, own, LANES), F32)
    return pl.pallas_call(
        fold_kernel,
        in_specs=[pl.BlockSpec(memory_space=pltpu.SMEM), pl.BlockSpec(memory_space=pl.ANY)],
        out_specs=(vmem, vmem),
        out_shape=(out, out),
        scratch_shapes=[
            pltpu.VMEM((parts.shape[0], terms, SUB, LANES), BF),
            pltpu.VMEM((terms, 2, own, LANES), F32),
            pltpu.SemaphoreType.DMA,
        ],
        compiler_params=params(16),
    )(place, in_hbm(parts))


def finish_kernel(devices, scale, place_ref, tiles_ref, a_ref, b_ref, c_ref, d_ref, *refs):
    left_ref, right_ref, near, far = refs
    near[...] = a_ref[...] + b_ref[...]
    far[...] = c_ref[...] + d_ref[...]
    count = tiles_ref.shape[0]
    row = place_ref[1] // (devices // count)
    lower = place_ref[1] < devices // 2
    start = jnp.where(lower, 0, count - row)

    def write(left, right):
        for tile in range(count):
            lanes = slice(tile * LANES, (tile + 1) * LANES)
            factor = tiles_ref[row, tile].astype(F32) * scale
            at = jnp.minimum(start + tile, count)
            left_ref[:, lanes] = left[at] * factor
            right_ref[:, lanes] = right[at] * factor

    @pl.when(lower)
    def _():
        write(near, far)

    @pl.when(jnp.logical_not(lower))
    def _():
        write(far, near)


def finish(place, tiles, pieces, devices, scale):
    terms, own, _ = pieces[0].shape
    smem = pl.BlockSpec(memory_space=pltpu.SMEM)
    vmem = pl.BlockSpec(memory_space=pltpu.VMEM)
    out = shape((own, (terms - 1) * LANES), F32)
    slab = pltpu.VMEM((terms, own, LANES), F32)
    return pl.pallas_call(
        lambda *refs: finish_kernel(devices, scale, *refs),
        in_specs=[smem, smem] + [vmem] * 4,
        out_specs=(vmem, vmem),
        out_shape=(out, out),
        scratch_shapes=[slab, slab],
        compiler_params=params(16),
    )(place, tiles, *pieces)


def swap(x):
    return lax.all_to_all(x, "seq", split_axis=0, concat_axis=0, tiled=True)


def shards(inputs, gate_in, cotangent, right_factor, left_factor, mask_tiles):
    width = right_factor.shape[0]
    rows, channels = inputs.shape[1], inputs.shape[2]
    seq_count = lax.axis_size("seq")
    data_count = lax.axis_size("dp")
    own = width // (seq_count * data_count)
    place = jnp.stack((lax.axis_index("dp"), lax.axis_index("seq"))).astype(jnp.int32)

    parts, place = spread(place, inputs, cotangent, gate_in)
    parts = swap(parts)
    mixed, grad_first, right, keep, give = mix(
        place, mask_tiles, left_factor, right_factor, parts, own
    )
    got = lax.ppermute(give, "dp", [(d, d ^ 1) for d in range(data_count)])
    parts = back(right, grad_first, mixed, rows)
    parts = add(keep, got, parts)
    parts = swap(parts)
    mine, other = fold(place, parts, mask_tiles.shape[0] + 1, own)

    def move(x, mirror, flip):
        pairs = [
            (
                s * data_count + d,
                (seq_count - 1 - s if mirror else s) * data_count + (d ^ flip),
            )
            for s in range(seq_count)
            for d in range(data_count)
        ]
        return lax.ppermute(x, ("seq", "dp"), pairs)

    pieces = (mine, move(other, False, 2), move(mine, True, 0), move(other, True, 2))
    grad_input, grad_gate = gather(parts, cotangent, gate_in, mine)
    scale = 1.0 / math.sqrt(data_count * channels * width)
    grad_left, grad_right = finish(place, mask_tiles, pieces, seq_count, scale)
    return grad_input, grad_gate, grad_right, grad_left


def solution(mesh):
    placed = (
        P("dp", "seq", None, None),
        P("dp", "seq", None, None),
        P("dp", "seq", None, None),
        P(),
        P(),
        P(),
    )
    return jax.shard_map(
        shards,
        mesh=mesh,
        in_specs=placed,
        out_specs=(
            P("dp", "seq", None, None),
            P("dp", "seq", None, None),
            P(("seq", "dp"), None),
            P(("seq", "dp"), None),
        ),
        check_vma=False,
    )
```

```python
import math

import jax
import jax.numpy as jnp
from jax import lax
from jax.experimental import pallas as pl
from jax.experimental.pallas import tpu as pltpu
from jax.sharding import PartitionSpec as P

BF = jnp.bfloat16
F32 = jnp.float32
MIB = 1024 * 1024
LANES = 128
SUB = 16
SIDE = 256


def params(mib):
    return pltpu.CompilerParams(vmem_limit_bytes=mib * MIB)


def shape(dims, dtype):
    return jax.ShapeDtypeStruct(dims, dtype)


def in_hbm(x):
    return pltpu.with_memory_space_constraint(x, pltpu.HBM)


def dot(a, b, on_a, on_b):
    return lax.dot_general(a, b, (((on_a,), (on_b,)), ((), ())), preferred_element_type=F32)


class Copies:
    def __init__(self, sems):
        self.sems, self.all, self.begun = sems, [], 0

    def add(self, src, dst):
        self.all.append(pltpu.make_async_copy(src, dst, self.sems.at[len(self.all)]))
        return len(self.all) - 1

    def begin(self, count):
        for copy in self.all[self.begun : count]:
            copy.start()
        self.begun = max(self.begun, min(count, len(self.all)))

    def start(self, src, dst):
        self.add(src, dst)
        self.begin(len(self.all))

    def take(self, index, ahead=0):
        self.begin(index + 1 + ahead)
        self.all[index].wait()

    def wait(self):
        for copy in self.all:
            copy.wait()


def put_tiles(ref, lead, part, rows, first_tile, tiles):
    devices, halves = part.shape[0] // rows, rows // SUB
    for tile in range(part.shape[1] // LANES):
        piece = part[:, tile * LANES : (tile + 1) * LANES].reshape(devices, halves, SUB, LANES)
        for half in range(halves):
            at = half * tiles + first_tile + tile
            ref[lead : lead + devices, at] = piece[:, half]


def turning():
    size = SUB * SUB
    row = lax.broadcasted_iota(jnp.int32, (size, size), 0)
    col = lax.broadcasted_iota(jnp.int32, (size, size), 1)
    return jnp.where(col == row % SUB * SUB + row // SUB, 1.0, 0.0).astype(BF)


def chunks_of(rows, channels):
    for group in range(channels // SUB):
        devices = pl.ds(group * SUB // 2, SUB // 2)
        for half in range(rows // SUB):
            yield half, pl.ds(half * SUB, SUB), pl.ds(group * SUB, SUB), devices


def spread_kernel(
    place_ref, x_hbm, cot_hbm, gate_hbm, out_hbm, place_out_ref,
    x, cot, gate, out, in_sems, out_sems,
):
    for k in range(place_ref.shape[0]):
        place_out_ref[k] = place_ref[k]
    _, rows, channels, width = x.shape
    size, dims = SUB * SUB, (SUB // 2, 2, SUB, width)
    loads, stores = Copies(in_sems), Copies(out_sems)
    chunks, turned = list(chunks_of(rows, channels)), turning()
    for _, at, group, _ in chunks:
        for src, dst in ((x_hbm, x), (cot_hbm, cot), (gate_hbm, gate)):
            loads.add(src.at[0, at, group], dst.at[0, at, group])
    loads.begin(len(loads.all))
    for k, (_, at, group, devices) in enumerate(chunks):
        for copy in range(3):
            loads.take(3 * k + copy)
        part = dot(turned, x[0, at, group].reshape(size, width), 1, 0)
        out[devices, :, 0, at] = part.astype(BF).reshape(dims)
        tanh = jnp.tanh(gate[0, at, group].astype(F32) * 0.5)
        grad = (cot[0, at, group].astype(F32) * (0.5 + 0.5 * tanh)).astype(BF)
        part = dot(turned, grad.reshape(size, width), 1, 0)
        out[devices, :, 1, at] = part.astype(BF).reshape(dims)
        stores.start(out.at[devices, :, :, at], out_hbm.at[devices, :, :, at])
    stores.wait()


def spread(place, x, cot, gate):
    _, rows, channels, width = x.shape
    smem = pl.BlockSpec(memory_space=pltpu.SMEM)
    whole = pl.BlockSpec(memory_space=pl.ANY)
    dims = (channels // 2, 2, 2, rows, width)
    count = rows * channels // (SUB * SUB)
    return pl.pallas_call(
        spread_kernel,
        in_specs=[smem] + [whole] * 3,
        out_specs=(whole, smem),
        out_shape=(pltpu.HBM(dims, BF), shape(place.shape, place.dtype)),
        scratch_shapes=[pltpu.VMEM(x.shape, BF)] * 3
        + [
            pltpu.VMEM(dims, BF),
            pltpu.SemaphoreType.DMA((3 * count,)),
            pltpu.SemaphoreType.DMA((count,)),
        ],
        compiler_params=params(48),
    )(place, in_hbm(x), in_hbm(cot), in_hbm(gate))


def gather_kernel(
    lead_hbm, in_hbm_ref, cot_hbm, gate_hbm, after_ref, back_hbm, grad_hbm,
    ahead, parts, cot, gate, back, grad, in_sems, out_sems,
):
    _, rows, channels, width = cot.shape
    size, dims = SUB * SUB, (SUB, SUB, width)
    tiles, halves = width // LANES, rows // SUB
    loads, stores = Copies(in_sems), Copies(out_sems)
    chunks, turned = list(chunks_of(rows, channels)), turning()

    def tiles_at(half, k):
        return pl.ds((k * halves + half) * tiles, tiles)

    for half, at, group, devices in chunks:
        where = (devices, tiles_at(half, 0))
        loads.add(lead_hbm.at[where], ahead.at[where])
        for k in range(3):
            where = (devices, tiles_at(half, k))
            loads.add(in_hbm_ref.at[where], parts.at[where])
        for src, dst in ((cot_hbm, cot), (gate_hbm, gate)):
            loads.add(src.at[0, at, group], dst.at[0, at, group])

    def rows_of(both, half, devices):
        columns = []
        for tile in range(tiles):
            pair = [ref[devices, (k * halves + half) * tiles + tile] for ref, k in both]
            columns.append(jnp.stack(pair, 1).reshape(size, LANES))
        return dot(turned, jnp.concatenate(columns, 1), 1, 0)

    loads.begin(len(loads.all))
    for k, (half, at, group, devices) in enumerate(chunks):
        for copy in range(6):
            loads.take(6 * k + copy)
        part = rows_of(((parts, 1), (parts, 2)), half, devices)
        back[0, at, group] = part.astype(BF).reshape(dims)
        stores.start(back.at[0, at, group], back_hbm.at[0, at, group])
        mixed = rows_of(((ahead, 0), (parts, 0)), half, devices).reshape(dims)
        tanh = jnp.tanh(gate[0, at, group].astype(F32) * 0.5)
        slope = 0.25 * (1.0 - tanh) * (1.0 + tanh)
        grad[0, at, group] = (cot[0, at, group].astype(F32) * mixed * slope).astype(BF)
        stores.start(grad.at[0, at, group], grad_hbm.at[0, at, group])
    stores.wait()


def gather(ahead, parts, cot, gate, after):
    _, rows, channels, width = cot.shape
    whole = pl.BlockSpec(memory_space=pl.ANY)
    devices, blocks = ahead.shape[:2]
    count = rows * channels // (SUB * SUB)
    natural = pltpu.VMEM(cot.shape, BF)
    return pl.pallas_call(
        gather_kernel,
        in_specs=[whole] * 5,
        out_specs=(whole, whole),
        out_shape=(pltpu.HBM(cot.shape, BF), pltpu.HBM(cot.shape, BF)),
        scratch_shapes=[
            pltpu.VMEM(ahead.shape, BF),
            pltpu.VMEM((devices, 3 * blocks, SUB, LANES), BF),
            natural,
            natural,
            natural,
            natural,
            pltpu.SemaphoreType.DMA((6 * count,)),
            pltpu.SemaphoreType.DMA((2 * count,)),
        ],
        compiler_params=params(48),
    )(in_hbm(ahead), in_hbm(parts), in_hbm(cot), in_hbm(gate), after)


def mask_factor(tiles_ref, ref, begin):
    count = tiles_ref.shape[0]
    side = ref.shape[0] // count
    for a in range(begin // side, (begin + SIDE) // side):
        for b in range((begin + SIDE) // side):
            where = (slice(a * side, (a + 1) * side), slice(b * side, (b + 1) * side))
            if b > a:
                ref[where] = jnp.zeros((side, side), BF)
            else:
                keep = jnp.full((side, side), tiles_ref[a, b].astype(F32)).astype(BF)
                ref[where] = ref[where] * keep


def blocks_of(width):
    return [(at, at + SIDE) for at in range(0, width, SIDE)]


def first_product(x, right, first):
    for at, end in blocks_of(x.shape[0]):
        first[:, at:end] = dot(x[:, :end], right[at:end, :end], 1, 1).astype(BF)


def mixed_product(left, first, mixed, rows):
    for at, end in blocks_of(left.shape[0]):
        part = dot(left[at:end, :end], first[:end], 1, 0).astype(BF)
        put_tiles(mixed, at // rows, part, rows, 0, part.shape[1] // LANES)


def lead_kernel(
    tiles_ref, left_hbm, right_hbm, parts_hbm, out_hbm, first_hbm,
    left, right, x, first, mixed, in_sems, out_sems,
):
    width, rows = left.shape[0], x.shape[1]
    blocks = blocks_of(width)
    loads, stores = Copies(in_sems), Copies(out_sems)

    count = len(blocks)

    def strip_of(src, dst, at, end):
        strip = (pl.ds(at, SIDE), pl.ds(0, end))
        loads.add(src.at[strip], dst.at[strip])

    for at, end in blocks:
        strip_of(right_hbm, right, at, end)
    for at, end in blocks:
        devices = pl.ds(at // rows, SIDE // rows)
        loads.add(parts_hbm.at[devices, 0, 0], x.at[devices])
    for at, end in blocks:
        strip_of(left_hbm, left, at, end)
    loads.begin(2 * count)
    for k, (at, _) in enumerate(blocks):
        loads.take(k)
        mask_factor(tiles_ref, right, at)
    loads.begin(3 * count)
    for k, (begin, stop) in enumerate(blocks):
        loads.take(count + k)
        strip = x[begin // rows : stop // rows].reshape(SIDE, width)
        for at, end in blocks:
            part = dot(strip[:, :end], right[at:end, :end], 1, 1)
            first[begin:stop, at:end] = part.astype(BF)
        stores.start(first.at[pl.ds(begin, SIDE)], first_hbm.at[pl.ds(begin, SIDE)])
    for k, (at, end) in enumerate(blocks):
        loads.take(2 * count + k)
        mask_factor(tiles_ref, left, at)
        part = dot(left[at:end, :end], first[:end], 1, 0).astype(BF)
        put_tiles(mixed, at // rows, part, rows, 0, width // LANES)
        devices = pl.ds(at // rows, SIDE // rows)
        stores.start(mixed.at[devices], out_hbm.at[devices])
    stores.wait()


def lead(tiles, left, right, parts):
    devices, _, _, rows, width = parts.shape
    whole = pl.BlockSpec(memory_space=pl.ANY)
    square = pltpu.VMEM((width, width), BF)
    dims = (devices, rows * width // (SUB * LANES), SUB, LANES)
    return pl.pallas_call(
        lead_kernel,
        in_specs=[pl.BlockSpec(memory_space=pltpu.SMEM), whole, whole, whole],
        out_specs=(whole, whole),
        out_shape=(pltpu.HBM(dims, BF), pltpu.HBM((width, width), BF)),
        scratch_shapes=[
            square,
            square,
            pltpu.VMEM((devices, rows, width), BF),
            square,
            pltpu.VMEM(dims, BF),
            pltpu.SemaphoreType.DMA((3 * width // SIDE,)),
            pltpu.SemaphoreType.DMA((2 * width // SIDE,)),
        ],
        compiler_params=params(32),
    )(tiles, in_hbm(left), in_hbm(right), in_hbm(parts))


def rest_kernel(
    place_ref, tiles_ref, left_hbm, right_hbm, parts_hbm, first_hbm,
    out_hbm, keep_hbm, give_hbm,
    left, right, xs, gs, first, grad, outs, total, keep, give, in_sems, out_sems,
):
    width, rows = left.shape[0], xs.shape[2]
    devices = width // rows
    loads, stores = Copies(in_sems), Copies(out_sems)
    blocks = blocks_of(width)
    for at, end in reversed(blocks):
        strip = (pl.ds(at, SIDE), pl.ds(0, end))
        loads.add(left_hbm.at[strip], left.at[strip])
        devices_at = pl.ds(at // rows, SIDE // rows)
        loads.add(parts_hbm.at[devices_at, 0, 1], gs.at[0, devices_at])
    strips = len(loads.all)
    loads.add(parts_hbm.at[:, 1, 1], gs.at[1])
    loads.add(right_hbm, right)
    loads.add(parts_hbm.at[:, 1, 0], xs.at[1])
    loads.add(first_hbm, first.at[0])
    loads.add(parts_hbm.at[:, 0, 0], xs.at[0])

    def send(k, begin=0, stop=devices):
        where, count = pl.ds(begin, stop - begin), outs.shape[2]
        stores.start(outs.at[k, where], out_hbm.at[where, pl.ds(k * count, count)])

    for c in range(2):
        loads.begin(strips + 2 * c + 1)
        if c == 1:
            loads.take(strips)
        for k, (at, end) in enumerate(reversed(blocks)):
            if c == 0:
                loads.take(2 * k)
                loads.take(2 * k + 1)
                mask_factor(tiles_ref, left, at)
            g = gs[c, at // rows :].reshape(width - at, width)
            grad[c, at:end] = dot(left[at:, at:end], g, 0, 0).astype(BF)
    loads.begin(len(loads.all))
    loads.take(strips + 1)
    for at, _ in blocks:
        mask_factor(tiles_ref, right, at)
    loads.take(strips + 2)
    first_product(xs[1].reshape(width, width), right, first.at[1])
    mixed_product(left, first.at[1], outs.at[0], rows)
    send(0)
    loads.take(strips + 3)
    loads.take(strips + 4)

    core = place_ref[0] % 2
    side = width // tiles_ref.shape[0]
    per_tile = devices * side // width
    for at, end in blocks_of(width):
        sums = [None, None]
        for c in range(2):
            x, g = xs[c].reshape(width, width), gs[c].reshape(width, width)
            left_part = dot(g[at:end], first[c, :end], 1, 1)
            right_part = dot(grad[c, :, at:end], x[:, :end], 0, 0)
            for k, part in enumerate((left_part, right_part)):
                sums[k] = part if sums[k] is None else sums[k] + part
        for k in range(2):
            total[k, :, :, :, :, :end] = sums[k].reshape(total.shape[1:5] + (end,))
        for s in range(at // rows, end // rows):
            lower = s < devices // 2
            mirror = devices - 1 - s
            first_tile = 0 if lower else (mirror // per_tile) + 1
            for k in range(2):
                to = (s if lower else mirror) if k == 0 else (mirror if lower else s)
                for tile in range(s // per_tile + 1):
                    cols = slice(tile * LANES, (tile + 1) * LANES)
                    place = first_tile + tile
                    own = total[k, s - at // rows, :, core, :, cols]
                    keep[to, place] = own.reshape(SUB, LANES)
                    other = total[k, s - at // rows, :, 1 - core, :, cols]
                    give[to, place] = other.reshape(SUB, LANES).astype(BF)
    stores.start(keep, keep_hbm)
    stores.start(give, give_hbm)

    for c in range(2):
        for begin, stop in blocks:
            for at, end in blocks:
                part = dot(grad[c, begin:stop, at:], right[at:, at:end], 1, 0).astype(BF)
                lead_device = begin // rows
                put_tiles(outs.at[1 + c], lead_device, part, rows, at // LANES, width // LANES)
            send(1 + c, begin // rows, stop // rows)
    stores.wait()


def rest(place, tiles, left, right, parts, first, own):
    devices, _, _, rows, width = parts.shape
    halves = rows // SUB
    count = width // LANES * halves
    terms = tiles.shape[0] + 1
    smem = pl.BlockSpec(memory_space=pltpu.SMEM)
    whole = pl.BlockSpec(memory_space=pl.ANY)
    square = pltpu.VMEM((width, width), BF)
    channels = pltpu.VMEM((2, devices, rows, width), BF)
    squares = pltpu.VMEM((2, width, width), BF)
    dims = (devices, terms, SUB, LANES)
    return pl.pallas_call(
        rest_kernel,
        in_specs=[smem, smem] + [whole] * 4,
        out_specs=(whole,) * 3,
        out_shape=(
            pltpu.HBM((devices, 3 * count + terms, SUB, LANES), BF),
            pltpu.HBM(dims, F32),
            pltpu.HBM(dims, BF),
        ),
        scratch_shapes=[
            square,
            square,
            channels,
            channels,
            squares,
            squares,
            pltpu.VMEM((3, devices, count, SUB, LANES), BF),
            pltpu.VMEM((2, SIDE // rows, halves, 2, own, width), F32),
            pltpu.VMEM(dims, F32),
            pltpu.VMEM(dims, BF),
            pltpu.SemaphoreType.DMA((5 + 2 * width // SIDE,)),
            pltpu.SemaphoreType.DMA((3 + 2 * width // SIDE,)),
        ],
        compiler_params=params(56),
    )(place, tiles, in_hbm(left), in_hbm(right), in_hbm(parts), in_hbm(first))


def add_kernel(keep_ref, got_ref, parts_ref, out_ref, total, sem):
    total[...] = (keep_ref[...] + got_ref[...].astype(F32)).astype(BF)
    terms = total.shape[1]
    copy = pltpu.make_async_copy(
        total, out_ref.at[:, pl.ds(out_ref.shape[1] - terms, terms)], sem
    )
    copy.start()
    copy.wait()


def add(keep, got, parts):
    vmem = pl.BlockSpec(memory_space=pltpu.VMEM)
    whole = pl.BlockSpec(memory_space=pl.ANY)
    return pl.pallas_call(
        add_kernel,
        in_specs=[vmem, vmem, whole],
        out_specs=whole,
        out_shape=pltpu.HBM(parts.shape, BF),
        input_output_aliases={2: 0},
        scratch_shapes=[pltpu.VMEM(keep.shape, BF), pltpu.SemaphoreType.DMA],
        compiler_params=params(16),
    )(keep, got, in_hbm(parts))


def tie_kernel(parts_ref, after_ref, out_ref):
    pass


def tie(parts, after):
    whole = pl.BlockSpec(memory_space=pl.ANY)
    return pl.pallas_call(
        tie_kernel,
        in_specs=[whole, whole],
        out_specs=whole,
        out_shape=pltpu.HBM(parts.shape, BF),
        input_output_aliases={0: 0},
    )(in_hbm(parts), after)


def fold_kernel(parts_ref, out_ref, got, sem):
    _, terms, own, _ = out_ref.shape
    copy = pltpu.make_async_copy(
        parts_ref.at[:, pl.ds(parts_ref.shape[1] - terms, terms)], got, sem
    )
    copy.start()
    copy.wait()
    total = jnp.sum(got[...].astype(F32), 0).reshape(terms, 2, own, LANES)
    for k in range(4):
        out_ref[k] = total[:, k % 2]


def fold(parts, terms, own):
    return pl.pallas_call(
        fold_kernel,
        in_specs=[pl.BlockSpec(memory_space=pl.ANY)],
        out_specs=pl.BlockSpec(memory_space=pltpu.VMEM),
        out_shape=shape((4, terms, own, LANES), F32),
        scratch_shapes=[
            pltpu.VMEM((parts.shape[0], terms, SUB, LANES), BF),
            pltpu.SemaphoreType.DMA,
        ],
        compiler_params=params(16),
    )(in_hbm(parts))


def finish_kernel(devices, scale, place_ref, tiles_ref, got_ref, left_ref, right_ref, total):
    count = tiles_ref.shape[0]
    total[0] = got_ref[0] + got_ref[1]
    total[1] = got_ref[2] + got_ref[3]
    row = place_ref[1] // (devices // count)
    start = jnp.where(place_ref[1] < devices // 2, 0, count - row)
    for tile in range(count):
        lanes = slice(tile * LANES, (tile + 1) * LANES)
        factor = tiles_ref[row, tile].astype(F32) * scale
        at = jnp.minimum(start + tile, count)
        left_ref[:, lanes] = total[0, at] * factor
        right_ref[:, lanes] = total[1, at] * factor


def finish(place, tiles, got, devices, scale):
    _, terms, own, _ = got.shape
    smem = pl.BlockSpec(memory_space=pltpu.SMEM)
    vmem = pl.BlockSpec(memory_space=pltpu.VMEM)
    out = shape((own, (terms - 1) * LANES), F32)
    return pl.pallas_call(
        lambda *refs: finish_kernel(devices, scale, *refs),
        in_specs=[smem, smem, vmem],
        out_specs=(vmem, vmem),
        out_shape=(out, out),
        scratch_shapes=[pltpu.VMEM((2, terms, own, LANES), F32)],
        compiler_params=params(16),
    )(place, tiles, got)


def swap(x):
    return lax.all_to_all(x, "seq", split_axis=0, concat_axis=0, tiled=True)


def shards(inputs, gate_in, cotangent, right_factor, left_factor, mask_tiles):
    width = right_factor.shape[0]
    rows, channels = inputs.shape[1], inputs.shape[2]
    seq_count = lax.axis_size("seq")
    data_count = lax.axis_size("dp")
    own = width // (seq_count * data_count)
    place = jnp.stack((lax.axis_index("dp"), lax.axis_index("seq"))).astype(jnp.int32)

    parts, place = spread(place, inputs, cotangent, gate_in)
    parts = swap(parts)
    ahead, first = lead(mask_tiles, left_factor, right_factor, parts)
    ahead = swap(ahead)
    parts, keep, give = rest(
        place, mask_tiles, left_factor, right_factor, parts, first, own
    )
    got = lax.ppermute(give, "dp", [(d, d ^ 1) for d in range(data_count)])
    parts = swap(tie(add(keep, got, parts), ahead))
    sums = fold(parts, mask_tiles.shape[0] + 1, own)
    groups = [
        [at * data_count + d for at in (s, seq_count - 1 - s) for d in (core, core + 2)]
        for s in range(seq_count // 2)
        for core in range(2)
    ]
    got = lax.all_to_all(
        sums,
        ("seq", "dp"),
        split_axis=0,
        concat_axis=0,
        tiled=True,
        axis_index_groups=groups,
    )
    grad_input, grad_gate = gather(ahead, parts, cotangent, gate_in, sums)
    scale = 1.0 / math.sqrt(data_count * channels * width)
    grad_left, grad_right = finish(place, mask_tiles, got, seq_count, scale)
    return grad_input, grad_gate, grad_right, grad_left


def solution(mesh):
    placed = (
        P("dp", "seq", None, None),
        P("dp", "seq", None, None),
        P("dp", "seq", None, None),
        P(),
        P(),
        P(),
    )
    return jax.shard_map(
        shards,
        mesh=mesh,
        in_specs=placed,
        out_specs=(
            P("dp", "seq", None, None),
            P("dp", "seq", None, None),
            P(("seq", "dp"), None),
            P(("seq", "dp"), None),
        ),
        check_vma=False,
    )
```

```python
import math

import jax
import jax.numpy as jnp
from jax import lax
from jax.experimental import pallas as pl
from jax.experimental.pallas import tpu as pltpu
from jax.sharding import PartitionSpec as P

BF = jnp.bfloat16
F32 = jnp.float32
MIB = 1024 * 1024
LANES = 128
SUB = 16
SIDE = 256


def params(mib):
    return pltpu.CompilerParams(vmem_limit_bytes=mib * MIB)


def shape(dims, dtype):
    return jax.ShapeDtypeStruct(dims, dtype)


def in_hbm(x):
    return pltpu.with_memory_space_constraint(x, pltpu.HBM)


def dot(a, b, on_a, on_b):
    return lax.dot_general(a, b, (((on_a,), (on_b,)), ((), ())), preferred_element_type=F32)


class Copies:
    def __init__(self, sems):
        self.sems, self.all, self.begun = sems, [], 0

    def add(self, src, dst):
        self.all.append(pltpu.make_async_copy(src, dst, self.sems.at[len(self.all)]))
        return len(self.all) - 1

    def begin(self, count):
        for copy in self.all[self.begun : count]:
            copy.start()
        self.begun = max(self.begun, min(count, len(self.all)))

    def start(self, src, dst):
        self.add(src, dst)
        self.begin(len(self.all))

    def take(self, index, ahead=0):
        self.begin(index + 1 + ahead)
        self.all[index].wait()

    def wait(self):
        for copy in self.all:
            copy.wait()


def put_tiles(ref, lead, part, rows, first_tile, tiles):
    devices, halves = part.shape[0] // rows, rows // SUB
    for tile in range(part.shape[1] // LANES):
        piece = part[:, tile * LANES : (tile + 1) * LANES].reshape(devices, halves, SUB, LANES)
        for half in range(halves):
            at = half * tiles + first_tile + tile
            ref[lead : lead + devices, at] = piece[:, half]


def turning():
    size = SUB * SUB
    row = lax.broadcasted_iota(jnp.int32, (size, size), 0)
    col = lax.broadcasted_iota(jnp.int32, (size, size), 1)
    return jnp.where(col == row % SUB * SUB + row // SUB, 1.0, 0.0).astype(BF)


def chunks_of(rows, channels):
    for group in range(channels // SUB):
        devices = pl.ds(group * SUB // 2, SUB // 2)
        for half in range(rows // SUB):
            yield half, pl.ds(half * SUB, SUB), pl.ds(group * SUB, SUB), devices


def spread_kernel(
    place_ref, x_hbm, cot_hbm, gate_hbm, out_hbm, place_out_ref,
    x, cot, gate, out, in_sems, out_sems,
):
    for k in range(place_ref.shape[0]):
        place_out_ref[k] = place_ref[k]
    _, rows, channels, width = x.shape
    size, dims = SUB * SUB, (SUB // 2, 2, SUB, width)
    loads, stores = Copies(in_sems), Copies(out_sems)
    chunks, turned = list(chunks_of(rows, channels)), turning()
    for _, at, group, _ in chunks:
        for src, dst in ((x_hbm, x), (cot_hbm, cot), (gate_hbm, gate)):
            loads.add(src.at[0, at, group], dst.at[0, at, group])
    loads.begin(len(loads.all))
    for k, (_, at, group, devices) in enumerate(chunks):
        for copy in range(3):
            loads.take(3 * k + copy)
        part = dot(turned, x[0, at, group].reshape(size, width), 1, 0)
        out[devices, :, 0, at] = part.astype(BF).reshape(dims)
        tanh = jnp.tanh(gate[0, at, group].astype(F32) * 0.5)
        grad = (cot[0, at, group].astype(F32) * (0.5 + 0.5 * tanh)).astype(BF)
        part = dot(turned, grad.reshape(size, width), 1, 0)
        out[devices, :, 1, at] = part.astype(BF).reshape(dims)
        stores.start(out.at[devices, :, :, at], out_hbm.at[devices, :, :, at])
    stores.wait()


def spread(place, x, cot, gate):
    _, rows, channels, width = x.shape
    smem = pl.BlockSpec(memory_space=pltpu.SMEM)
    whole = pl.BlockSpec(memory_space=pl.ANY)
    dims = (channels // 2, 2, 2, rows, width)
    count = rows * channels // (SUB * SUB)
    return pl.pallas_call(
        spread_kernel,
        in_specs=[smem] + [whole] * 3,
        out_specs=(whole, smem),
        out_shape=(pltpu.HBM(dims, BF), shape(place.shape, place.dtype)),
        scratch_shapes=[pltpu.VMEM(x.shape, BF)] * 3
        + [
            pltpu.VMEM(dims, BF),
            pltpu.SemaphoreType.DMA((3 * count,)),
            pltpu.SemaphoreType.DMA((count,)),
        ],
        compiler_params=params(48),
    )(place, in_hbm(x), in_hbm(cot), in_hbm(gate))


def gather_kernel(
    lead_hbm, in_hbm_ref, cot_hbm, gate_hbm, after_ref, back_hbm, grad_hbm,
    ahead, parts, cot, gate, back, grad, in_sems, out_sems,
):
    _, rows, channels, width = cot.shape
    size, dims = SUB * SUB, (SUB, SUB, width)
    tiles, halves = width // LANES, rows // SUB
    loads, stores = Copies(in_sems), Copies(out_sems)
    chunks, turned = list(chunks_of(rows, channels)), turning()

    def tiles_at(half, k):
        return pl.ds((k * halves + half) * tiles, tiles)

    for half, at, group, devices in chunks:
        where = (devices, tiles_at(half, 0))
        loads.add(lead_hbm.at[where], ahead.at[where])
        for k in range(3):
            where = (devices, tiles_at(half, k))
            loads.add(in_hbm_ref.at[where], parts.at[where])
        for src, dst in ((cot_hbm, cot), (gate_hbm, gate)):
            loads.add(src.at[0, at, group], dst.at[0, at, group])

    def rows_of(both, half, devices):
        columns = []
        for tile in range(tiles):
            pair = [ref[devices, (k * halves + half) * tiles + tile] for ref, k in both]
            columns.append(jnp.stack(pair, 1).reshape(size, LANES))
        return dot(turned, jnp.concatenate(columns, 1), 1, 0)

    loads.begin(len(loads.all))
    for k, (half, at, group, devices) in enumerate(chunks):
        for copy in range(6):
            loads.take(6 * k + copy)
        part = rows_of(((parts, 1), (parts, 2)), half, devices)
        back[0, at, group] = part.astype(BF).reshape(dims)
        stores.start(back.at[0, at, group], back_hbm.at[0, at, group])
        mixed = rows_of(((ahead, 0), (parts, 0)), half, devices).reshape(dims)
        tanh = jnp.tanh(gate[0, at, group].astype(F32) * 0.5)
        slope = 0.25 * (1.0 - tanh) * (1.0 + tanh)
        grad[0, at, group] = (cot[0, at, group].astype(F32) * mixed * slope).astype(BF)
        stores.start(grad.at[0, at, group], grad_hbm.at[0, at, group])
    stores.wait()


def gather(ahead, parts, cot, gate, after):
    _, rows, channels, width = cot.shape
    whole = pl.BlockSpec(memory_space=pl.ANY)
    devices, blocks = ahead.shape[:2]
    count = rows * channels // (SUB * SUB)
    natural = pltpu.VMEM(cot.shape, BF)
    return pl.pallas_call(
        gather_kernel,
        in_specs=[whole] * 5,
        out_specs=(whole, whole),
        out_shape=(pltpu.HBM(cot.shape, BF), pltpu.HBM(cot.shape, BF)),
        scratch_shapes=[
            pltpu.VMEM(ahead.shape, BF),
            pltpu.VMEM((devices, 3 * blocks, SUB, LANES), BF),
            natural,
            natural,
            natural,
            natural,
            pltpu.SemaphoreType.DMA((6 * count,)),
            pltpu.SemaphoreType.DMA((2 * count,)),
        ],
        compiler_params=params(48),
    )(ahead, in_hbm(parts), cot, gate, after)


def mask_factor(tiles_ref, ref, begin):
    count = tiles_ref.shape[0]
    side = ref.shape[0] // count
    for a in range(begin // side, (begin + SIDE) // side):
        for b in range((begin + SIDE) // side):
            where = (slice(a * side, (a + 1) * side), slice(b * side, (b + 1) * side))
            if b > a:
                ref[where] = jnp.zeros((side, side), BF)
            else:
                keep = jnp.full((side, side), tiles_ref[a, b].astype(F32)).astype(BF)
                ref[where] = ref[where] * keep


def blocks_of(width):
    return [(at, at + SIDE) for at in range(0, width, SIDE)]


def first_product(x, right, first):
    for at, end in blocks_of(x.shape[0]):
        first[:, at:end] = dot(x[:, :end], right[at:end, :end], 1, 1).astype(BF)


def mixed_product(left, first, mixed, rows):
    for at, end in blocks_of(left.shape[0]):
        part = dot(left[at:end, :end], first[:end], 1, 0).astype(BF)
        put_tiles(mixed, at // rows, part, rows, 0, part.shape[1] // LANES)


def lead_kernel(
    tiles_ref, left_hbm, right_hbm, parts_hbm, out_hbm, first_hbm,
    left, right, x, first, mixed, in_sems, out_sems,
):
    width, rows = left.shape[0], x.shape[1]
    blocks = blocks_of(width)
    loads, stores = Copies(in_sems), Copies(out_sems)

    count = len(blocks)

    def strip_of(src, dst, at, end):
        strip = (pl.ds(at, SIDE), pl.ds(0, end))
        loads.add(src.at[strip], dst.at[strip])

    for at, end in blocks:
        strip_of(right_hbm, right, at, end)
    for at, end in blocks:
        devices = pl.ds(at // rows, SIDE // rows)
        loads.add(parts_hbm.at[devices, 0, 0], x.at[devices])
    for at, end in blocks:
        strip_of(left_hbm, left, at, end)
    loads.begin(2 * count)
    for k, (at, _) in enumerate(blocks):
        loads.take(k)
        mask_factor(tiles_ref, right, at)
    loads.begin(3 * count)
    for k, (begin, stop) in enumerate(blocks):
        loads.take(count + k)
        strip = x[begin // rows : stop // rows].reshape(SIDE, width)
        for at, end in blocks:
            part = dot(strip[:, :end], right[at:end, :end], 1, 1)
            first[begin:stop, at:end] = part.astype(BF)
        stores.start(first.at[pl.ds(begin, SIDE)], first_hbm.at[pl.ds(begin, SIDE)])
    for k, (at, end) in enumerate(blocks):
        loads.take(2 * count + k)
        mask_factor(tiles_ref, left, at)
        part = dot(left[at:end, :end], first[:end], 1, 0).astype(BF)
        put_tiles(mixed, at // rows, part, rows, 0, width // LANES)
        devices = pl.ds(at // rows, SIDE // rows)
        stores.start(mixed.at[devices], out_hbm.at[devices])
    stores.wait()


def lead(tiles, left, right, parts):
    devices, _, _, rows, width = parts.shape
    whole = pl.BlockSpec(memory_space=pl.ANY)
    square = pltpu.VMEM((width, width), BF)
    dims = (devices, rows * width // (SUB * LANES), SUB, LANES)
    return pl.pallas_call(
        lead_kernel,
        in_specs=[pl.BlockSpec(memory_space=pltpu.SMEM), whole, whole, whole],
        out_specs=(whole, whole),
        out_shape=(pltpu.HBM(dims, BF), pltpu.HBM((width, width), BF)),
        scratch_shapes=[
            square,
            square,
            pltpu.VMEM((devices, rows, width), BF),
            square,
            pltpu.VMEM(dims, BF),
            pltpu.SemaphoreType.DMA((3 * width // SIDE,)),
            pltpu.SemaphoreType.DMA((2 * width // SIDE,)),
        ],
        compiler_params=params(32),
    )(tiles, left, right, in_hbm(parts))


def rest_kernel(
    place_ref, tiles_ref, left_hbm, right_hbm, parts_hbm, first_hbm,
    out_hbm, keep, give,
    left, right, xs, gs, first, grad, outs, total, in_sems, out_sems,
):
    width, rows = left.shape[0], xs.shape[2]
    devices = width // rows
    loads, stores = Copies(in_sems), Copies(out_sems)
    blocks = blocks_of(width)
    for at, end in reversed(blocks):
        strip = (pl.ds(at, SIDE), pl.ds(0, end))
        loads.add(left_hbm.at[strip], left.at[strip])
        devices_at = pl.ds(at // rows, SIDE // rows)
        loads.add(parts_hbm.at[devices_at, 0, 1], gs.at[0, devices_at])
    strips = len(loads.all)
    loads.add(parts_hbm.at[:, 1, 1], gs.at[1])
    loads.add(right_hbm, right)
    loads.add(parts_hbm.at[:, 1, 0], xs.at[1])
    loads.add(first_hbm, first.at[0])
    loads.add(parts_hbm.at[:, 0, 0], xs.at[0])

    def send(k, begin=0, stop=devices):
        where, count = pl.ds(begin, stop - begin), outs.shape[2]
        stores.start(outs.at[k, where], out_hbm.at[where, pl.ds(k * count, count)])

    for c in range(2):
        loads.begin(strips + 2 * c + 1)
        if c == 1:
            loads.take(strips)
        for k, (at, end) in enumerate(reversed(blocks)):
            if c == 0:
                loads.take(2 * k)
                loads.take(2 * k + 1)
                mask_factor(tiles_ref, left, at)
            g = gs[c, at // rows :].reshape(width - at, width)
            grad[c, at:end] = dot(left[at:, at:end], g, 0, 0).astype(BF)
    loads.begin(len(loads.all))
    loads.take(strips + 1)
    for at, _ in blocks:
        mask_factor(tiles_ref, right, at)
    loads.take(strips + 2)
    first_product(xs[1].reshape(width, width), right, first.at[1])
    mixed_product(left, first.at[1], outs.at[0], rows)
    send(0)
    loads.take(strips + 3)
    loads.take(strips + 4)

    core = place_ref[0] % 2
    side = width // tiles_ref.shape[0]
    per_tile = devices * side // width
    for at, end in blocks_of(width):
        sums = [None, None]
        for c in range(2):
            x, g = xs[c].reshape(width, width), gs[c].reshape(width, width)
            left_part = dot(g[at:end], first[c, :end], 1, 1)
            right_part = dot(grad[c, :, at:end], x[:, :end], 0, 0)
            for k, part in enumerate((left_part, right_part)):
                sums[k] = part if sums[k] is None else sums[k] + part
        for k in range(2):
            total[k, :, :, :, :, :end] = sums[k].reshape(total.shape[1:5] + (end,))
        for s in range(at // rows, end // rows):
            lower = s < devices // 2
            mirror = devices - 1 - s
            first_tile = 0 if lower else (mirror // per_tile) + 1
            for k in range(2):
                to = (s if lower else mirror) if k == 0 else (mirror if lower else s)
                for tile in range(s // per_tile + 1):
                    cols = slice(tile * LANES, (tile + 1) * LANES)
                    place = first_tile + tile
                    own = total[k, s - at // rows, :, core, :, cols]
                    keep[to, place] = own.reshape(SUB, LANES)
                    other = total[k, s - at // rows, :, 1 - core, :, cols]
                    give[to, place] = other.reshape(SUB, LANES).astype(BF)

    for c in range(2):
        for begin, stop in blocks:
            for at, end in blocks:
                part = dot(grad[c, begin:stop, at:], right[at:, at:end], 1, 0).astype(BF)
                lead_device = begin // rows
                put_tiles(outs.at[1 + c], lead_device, part, rows, at // LANES, width // LANES)
            send(1 + c, begin // rows, stop // rows)
    stores.wait()


def rest(place, tiles, left, right, parts, first, own):
    devices, _, _, rows, width = parts.shape
    halves = rows // SUB
    count = width // LANES * halves
    terms = tiles.shape[0] + 1
    smem = pl.BlockSpec(memory_space=pltpu.SMEM)
    whole = pl.BlockSpec(memory_space=pl.ANY)
    vmem = pl.BlockSpec(memory_space=pltpu.VMEM)
    square = pltpu.VMEM((width, width), BF)
    channels = pltpu.VMEM((2, devices, rows, width), BF)
    squares = pltpu.VMEM((2, width, width), BF)
    dims = (devices, terms, SUB, LANES)
    return pl.pallas_call(
        rest_kernel,
        in_specs=[smem, smem] + [whole] * 4,
        out_specs=(whole, vmem, vmem),
        out_shape=(
            pltpu.HBM((devices, 3 * count + terms, SUB, LANES), BF),
            pltpu.VMEM(dims, F32),
            pltpu.VMEM(dims, BF),
        ),
        scratch_shapes=[
            square,
            square,
            channels,
            channels,
            squares,
            squares,
            pltpu.VMEM((3, devices, count, SUB, LANES), BF),
            pltpu.VMEM((2, SIDE // rows, halves, 2, own, width), F32),
            pltpu.SemaphoreType.DMA((5 + 2 * width // SIDE,)),
            pltpu.SemaphoreType.DMA((1 + 2 * width // SIDE,)),
        ],
        compiler_params=params(56),
    )(place, tiles, in_hbm(left), in_hbm(right), in_hbm(parts), in_hbm(first))


def add_kernel(keep_ref, got_ref, parts_ref, out_ref, total, sem):
    total[...] = (keep_ref[...] + got_ref[...].astype(F32)).astype(BF)
    terms = total.shape[1]
    copy = pltpu.make_async_copy(
        total, out_ref.at[:, pl.ds(out_ref.shape[1] - terms, terms)], sem
    )
    copy.start()
    copy.wait()


def add(keep, got, parts):
    vmem = pl.BlockSpec(memory_space=pltpu.VMEM)
    whole = pl.BlockSpec(memory_space=pl.ANY)
    return pl.pallas_call(
        add_kernel,
        in_specs=[vmem, vmem, whole],
        out_specs=whole,
        out_shape=pltpu.HBM(parts.shape, BF),
        input_output_aliases={2: 0},
        scratch_shapes=[pltpu.VMEM(keep.shape, BF), pltpu.SemaphoreType.DMA],
        compiler_params=params(16),
    )(keep, got, in_hbm(parts))


def tie_kernel(parts_ref, after_ref, out_ref):
    pass


def tie(parts, after):
    whole = pl.BlockSpec(memory_space=pl.ANY)
    return pl.pallas_call(
        tie_kernel,
        in_specs=[whole, whole],
        out_specs=whole,
        out_shape=pltpu.HBM(parts.shape, BF),
        input_output_aliases={0: 0},
    )(in_hbm(parts), after)


def fold_kernel(parts_ref, out_ref, got, sem):
    _, terms, own, _ = out_ref.shape
    copy = pltpu.make_async_copy(
        parts_ref.at[:, pl.ds(parts_ref.shape[1] - terms, terms)], got, sem
    )
    copy.start()
    copy.wait()
    total = jnp.sum(got[...].astype(F32), 0).reshape(terms, 2, own, LANES)
    for k in range(4):
        out_ref[k] = total[:, k % 2]


def fold(parts, terms, own):
    return pl.pallas_call(
        fold_kernel,
        in_specs=[pl.BlockSpec(memory_space=pl.ANY)],
        out_specs=pl.BlockSpec(memory_space=pltpu.VMEM),
        out_shape=shape((4, terms, own, LANES), F32),
        scratch_shapes=[
            pltpu.VMEM((parts.shape[0], terms, SUB, LANES), BF),
            pltpu.SemaphoreType.DMA,
        ],
        compiler_params=params(16),
    )(in_hbm(parts))


def finish_kernel(devices, scale, place_ref, tiles_ref, got_ref, left_ref, right_ref, total):
    count = tiles_ref.shape[0]
    total[0] = got_ref[0] + got_ref[1]
    total[1] = got_ref[2] + got_ref[3]
    row = place_ref[1] // (devices // count)
    start = jnp.where(place_ref[1] < devices // 2, 0, count - row)
    for tile in range(count):
        lanes = slice(tile * LANES, (tile + 1) * LANES)
        factor = tiles_ref[row, tile].astype(F32) * scale
        at = jnp.minimum(start + tile, count)
        left_ref[:, lanes] = total[0, at] * factor
        right_ref[:, lanes] = total[1, at] * factor


def finish(place, tiles, got, devices, scale):
    _, terms, own, _ = got.shape
    smem = pl.BlockSpec(memory_space=pltpu.SMEM)
    vmem = pl.BlockSpec(memory_space=pltpu.VMEM)
    out = shape((own, (terms - 1) * LANES), F32)
    return pl.pallas_call(
        lambda *refs: finish_kernel(devices, scale, *refs),
        in_specs=[smem, smem, vmem],
        out_specs=(vmem, vmem),
        out_shape=(out, out),
        scratch_shapes=[pltpu.VMEM((2, terms, own, LANES), F32)],
        compiler_params=params(16),
    )(place, tiles, got)


def swap(x):
    return lax.all_to_all(x, "seq", split_axis=0, concat_axis=0, tiled=True)


def shards(inputs, gate_in, cotangent, right_factor, left_factor, mask_tiles):
    width = right_factor.shape[0]
    rows, channels = inputs.shape[1], inputs.shape[2]
    seq_count = lax.axis_size("seq")
    data_count = lax.axis_size("dp")
    own = width // (seq_count * data_count)
    place = jnp.stack((lax.axis_index("dp"), lax.axis_index("seq"))).astype(jnp.int32)

    parts, place = spread(place, inputs, cotangent, gate_in)
    parts = swap(parts)
    ahead, first = lead(mask_tiles, left_factor, right_factor, parts)
    ahead = swap(ahead)
    parts, keep, give = rest(
        place, mask_tiles, left_factor, right_factor, parts, first, own
    )
    got = lax.ppermute(give, "dp", [(d, d ^ 1) for d in range(data_count)])
    parts = swap(tie(add(keep, got, parts), ahead[0, 0]))
    sums = fold(parts, mask_tiles.shape[0] + 1, own)
    groups = [
        [at * data_count + d for at in (s, seq_count - 1 - s) for d in (core, core + 2)]
        for s in range(seq_count // 2)
        for core in range(2)
    ]
    got = lax.all_to_all(
        sums,
        ("seq", "dp"),
        split_axis=0,
        concat_axis=0,
        tiled=True,
        axis_index_groups=groups,
    )
    grad_input, grad_gate = gather(ahead, parts, cotangent, gate_in, sums)
    scale = 1.0 / math.sqrt(data_count * channels * width)
    grad_left, grad_right = finish(place, mask_tiles, got, seq_count, scale)
    return grad_input, grad_gate, grad_right, grad_left


def solution(mesh):
    placed = (
        P("dp", "seq", None, None),
        P("dp", "seq", None, None),
        P("dp", "seq", None, None),
        P(),
        P(),
        P(),
    )
    return jax.shard_map(
        shards,
        mesh=mesh,
        in_specs=placed,
        out_specs=(
            P("dp", "seq", None, None),
            P("dp", "seq", None, None),
            P(("seq", "dp"), None),
            P(("seq", "dp"), None),
        ),
        check_vma=False,
    )
```

```python
import math

import jax
import jax.numpy as jnp
from jax import lax
from jax.experimental import pallas as pl
from jax.experimental.pallas import tpu as pltpu
from jax.sharding import PartitionSpec as P

BF = jnp.bfloat16
F32 = jnp.float32
MIB = 1024 * 1024
LANES = 128
SUB = 16
SIDE = 256


def params(mib):
    return pltpu.CompilerParams(vmem_limit_bytes=mib * MIB)


def shape(dims, dtype):
    return jax.ShapeDtypeStruct(dims, dtype)


def in_hbm(x):
    return pltpu.with_memory_space_constraint(x, pltpu.HBM)


def dot(a, b, on_a, on_b):
    return lax.dot_general(a, b, (((on_a,), (on_b,)), ((), ())), preferred_element_type=F32)


class Copies:
    def __init__(self, sems):
        self.sems, self.all, self.begun = sems, [], 0

    def add(self, src, dst):
        self.all.append(pltpu.make_async_copy(src, dst, self.sems.at[len(self.all)]))
        return len(self.all) - 1

    def begin(self, count):
        for copy in self.all[self.begun : count]:
            copy.start()
        self.begun = max(self.begun, min(count, len(self.all)))

    def start(self, src, dst):
        self.add(src, dst)
        self.begin(len(self.all))

    def take(self, index, ahead=0):
        self.begin(index + 1 + ahead)
        self.all[index].wait()

    def wait(self):
        for copy in self.all:
            copy.wait()


def put_tiles(ref, lead, part, rows, first_tile, tiles):
    devices, halves = part.shape[0] // rows, rows // SUB
    for tile in range(part.shape[1] // LANES):
        piece = part[:, tile * LANES : (tile + 1) * LANES].reshape(devices, halves, SUB, LANES)
        for half in range(halves):
            at = half * tiles + first_tile + tile
            ref[lead : lead + devices, at] = piece[:, half]


def turning():
    size = SUB * SUB
    row = lax.broadcasted_iota(jnp.int32, (size, size), 0)
    col = lax.broadcasted_iota(jnp.int32, (size, size), 1)
    return jnp.where(col == row % SUB * SUB + row // SUB, 1.0, 0.0).astype(BF)


def chunks_of(rows, channels):
    for group in range(channels // SUB):
        devices = pl.ds(group * SUB // 2, SUB // 2)
        for half in range(rows // SUB):
            yield half, pl.ds(half * SUB, SUB), pl.ds(group * SUB, SUB), devices


def spread_kernel(
    place_ref, x_hbm, cot_hbm, gate_hbm, out, place_out_ref,
    x, cot, gate, in_sems,
):
    for k in range(place_ref.shape[0]):
        place_out_ref[k] = place_ref[k]
    _, rows, channels, width = x.shape
    size, dims = SUB * SUB, (SUB // 2, 2, SUB, width)
    loads = Copies(in_sems)
    chunks, turned = list(chunks_of(rows, channels)), turning()
    for _, at, group, _ in chunks:
        loads.add(x_hbm.at[0, at, group], x.at[0, at, group])
    for _, at, group, _ in chunks:
        for src, dst in ((cot_hbm, cot), (gate_hbm, gate)):
            loads.add(src.at[0, at, group], dst.at[0, at, group])
    count = len(chunks)
    loads.begin(count + 4)
    for k, (_, at, group, devices) in enumerate(chunks):
        loads.take(k)
        loads.begin(count + 6 + 2 * k)
        part = dot(turned, x[0, at, group].reshape(size, width), 1, 0)
        out[devices, :, 0, at] = part.astype(BF).reshape(dims)
    loads.begin(len(loads.all))
    for k, (_, at, group, devices) in enumerate(chunks):
        for copy in range(2):
            loads.take(count + 2 * k + copy)
        tanh = jnp.tanh(gate[0, at, group].astype(F32) * 0.5)
        grad = (cot[0, at, group].astype(F32) * (0.5 + 0.5 * tanh)).astype(BF)
        part = dot(turned, grad.reshape(size, width), 1, 0)
        out[devices, :, 1, at] = part.astype(BF).reshape(dims)


def spread(place, x, cot, gate):
    _, rows, channels, width = x.shape
    smem = pl.BlockSpec(memory_space=pltpu.SMEM)
    whole = pl.BlockSpec(memory_space=pl.ANY)
    dims = (channels // 2, 2, 2, rows, width)
    count = rows * channels // (SUB * SUB)
    return pl.pallas_call(
        spread_kernel,
        in_specs=[smem] + [whole] * 3,
        out_specs=(pl.BlockSpec(memory_space=pltpu.VMEM), smem),
        out_shape=(pltpu.VMEM(dims, BF), shape(place.shape, place.dtype)),
        scratch_shapes=[pltpu.VMEM(x.shape, BF)] * 3 + [pltpu.SemaphoreType.DMA((3 * count,))],
        compiler_params=params(48),
    )(place, in_hbm(x), in_hbm(cot), in_hbm(gate))


def gather_kernel(
    lead_hbm, in_hbm_ref, cot_hbm, gate_hbm, after_ref, back_hbm, grad_hbm,
    ahead, parts, cot, gate, back, grad, in_sems, out_sems,
):
    _, rows, channels, width = cot.shape
    size, dims = SUB * SUB, (SUB, SUB, width)
    tiles, halves = width // LANES, rows // SUB
    loads, stores = Copies(in_sems), Copies(out_sems)
    chunks, turned = list(chunks_of(rows, channels)), turning()

    def tiles_at(half, k):
        return pl.ds((k * halves + half) * tiles, tiles)

    for half, at, group, devices in chunks:
        where = (devices, tiles_at(half, 0))
        loads.add(lead_hbm.at[where], ahead.at[where])
        for k in range(3):
            where = (devices, tiles_at(half, k))
            loads.add(in_hbm_ref.at[where], parts.at[where])
        for src, dst in ((cot_hbm, cot), (gate_hbm, gate)):
            loads.add(src.at[0, at, group], dst.at[0, at, group])

    def rows_of(both, half, devices):
        columns = []
        for tile in range(tiles):
            pair = [ref[devices, (k * halves + half) * tiles + tile] for ref, k in both]
            columns.append(jnp.stack(pair, 1).reshape(size, LANES))
        return dot(turned, jnp.concatenate(columns, 1), 1, 0)

    loads.begin(len(loads.all))
    for k, (half, at, group, devices) in enumerate(chunks):
        for copy in range(6):
            loads.take(6 * k + copy)
        part = rows_of(((parts, 1), (parts, 2)), half, devices)
        back[0, at, group] = part.astype(BF).reshape(dims)
        stores.start(back.at[0, at, group], back_hbm.at[0, at, group])
        mixed = rows_of(((ahead, 0), (parts, 0)), half, devices).reshape(dims)
        tanh = jnp.tanh(gate[0, at, group].astype(F32) * 0.5)
        slope = 0.25 * (1.0 - tanh) * (1.0 + tanh)
        grad[0, at, group] = (cot[0, at, group].astype(F32) * mixed * slope).astype(BF)
        stores.start(grad.at[0, at, group], grad_hbm.at[0, at, group])
    stores.wait()


def gather(ahead, parts, cot, gate, after):
    _, rows, channels, width = cot.shape
    whole = pl.BlockSpec(memory_space=pl.ANY)
    devices, blocks = ahead.shape[:2]
    count = rows * channels // (SUB * SUB)
    natural = pltpu.VMEM(cot.shape, BF)
    return pl.pallas_call(
        gather_kernel,
        in_specs=[whole] * 5,
        out_specs=(whole, whole),
        out_shape=(pltpu.HBM(cot.shape, BF), pltpu.HBM(cot.shape, BF)),
        scratch_shapes=[
            pltpu.VMEM(ahead.shape, BF),
            pltpu.VMEM((devices, 3 * blocks, SUB, LANES), BF),
            natural,
            natural,
            natural,
            natural,
            pltpu.SemaphoreType.DMA((6 * count,)),
            pltpu.SemaphoreType.DMA((2 * count,)),
        ],
        compiler_params=params(48),
    )(ahead, in_hbm(parts), cot, gate, after)


def mask_factor(tiles_ref, ref, begin):
    count = tiles_ref.shape[0]
    side = ref.shape[0] // count
    for a in range(begin // side, (begin + SIDE) // side):
        for b in range((begin + SIDE) // side):
            where = (slice(a * side, (a + 1) * side), slice(b * side, (b + 1) * side))
            if b > a:
                ref[where] = jnp.zeros((side, side), BF)
            else:
                keep = jnp.full((side, side), tiles_ref[a, b].astype(F32)).astype(BF)
                ref[where] = ref[where] * keep


def blocks_of(width):
    return [(at, at + SIDE) for at in range(0, width, SIDE)]


def first_product(x, right, first):
    for at, end in blocks_of(x.shape[0]):
        first[:, at:end] = dot(x[:, :end], right[at:end, :end], 1, 1).astype(BF)


def mixed_product(left, first, mixed, rows):
    for at, end in blocks_of(left.shape[0]):
        part = dot(left[at:end, :end], first[:end], 1, 0).astype(BF)
        put_tiles(mixed, at // rows, part, rows, 0, part.shape[1] // LANES)


def lead_kernel(
    tiles_ref, left_hbm, right_hbm, parts_hbm, out_hbm, first_hbm,
    left, right, x, first, mixed, in_sems, out_sems,
):
    width, rows = left.shape[0], x.shape[1]
    blocks = blocks_of(width)
    loads, stores = Copies(in_sems), Copies(out_sems)

    count = len(blocks)

    def strip_of(src, dst, at, end):
        strip = (pl.ds(at, SIDE), pl.ds(0, end))
        loads.add(src.at[strip], dst.at[strip])

    for at, end in blocks:
        strip_of(right_hbm, right, at, end)
    for at, end in blocks:
        devices = pl.ds(at // rows, SIDE // rows)
        loads.add(parts_hbm.at[devices, 0, 0], x.at[devices])
    for at, end in blocks:
        strip_of(left_hbm, left, at, end)
    loads.begin(2 * count)
    for k, (at, _) in enumerate(blocks):
        loads.take(k)
        mask_factor(tiles_ref, right, at)
    loads.begin(3 * count)
    for k, (begin, stop) in enumerate(blocks):
        loads.take(count + k)
        strip = x[begin // rows : stop // rows].reshape(SIDE, width)
        for at, end in blocks:
            part = dot(strip[:, :end], right[at:end, :end], 1, 1)
            first[begin:stop, at:end] = part.astype(BF)
        stores.start(first.at[pl.ds(begin, SIDE)], first_hbm.at[pl.ds(begin, SIDE)])
    for k, (at, end) in enumerate(blocks):
        loads.take(2 * count + k)
        mask_factor(tiles_ref, left, at)
        part = dot(left[at:end, :end], first[:end], 1, 0).astype(BF)
        put_tiles(mixed, at // rows, part, rows, 0, width // LANES)
        devices = pl.ds(at // rows, SIDE // rows)
        stores.start(mixed.at[devices], out_hbm.at[devices])
    stores.wait()


def lead(tiles, left, right, parts):
    devices, _, _, rows, width = parts.shape
    whole = pl.BlockSpec(memory_space=pl.ANY)
    square = pltpu.VMEM((width, width), BF)
    dims = (devices, rows * width // (SUB * LANES), SUB, LANES)
    return pl.pallas_call(
        lead_kernel,
        in_specs=[pl.BlockSpec(memory_space=pltpu.SMEM), whole, whole, whole],
        out_specs=(whole, whole),
        out_shape=(pltpu.HBM(dims, BF), pltpu.HBM((width, width), BF)),
        scratch_shapes=[
            square,
            square,
            pltpu.VMEM((devices, rows, width), BF),
            square,
            pltpu.VMEM(dims, BF),
            pltpu.SemaphoreType.DMA((3 * width // SIDE,)),
            pltpu.SemaphoreType.DMA((2 * width // SIDE,)),
        ],
        compiler_params=params(32),
    )(tiles, left, right, in_hbm(parts))


def rest_kernel(
    place_ref, tiles_ref, left_hbm, right_hbm, parts_hbm, first_hbm,
    out_hbm, keep, give,
    left, right, xs, gs, first, grad, outs, total, in_sems, out_sems,
):
    width, rows = left.shape[0], xs.shape[2]
    devices = width // rows
    loads, stores = Copies(in_sems), Copies(out_sems)
    blocks = blocks_of(width)
    for at, end in reversed(blocks):
        strip = (pl.ds(at, SIDE), pl.ds(0, end))
        loads.add(left_hbm.at[strip], left.at[strip])
        devices_at = pl.ds(at // rows, SIDE // rows)
        loads.add(parts_hbm.at[devices_at, 0, 1], gs.at[0, devices_at])
    strips = len(loads.all)
    loads.add(parts_hbm.at[:, 1, 1], gs.at[1])
    loads.add(right_hbm, right)
    loads.add(parts_hbm.at[:, 1, 0], xs.at[1])
    loads.add(first_hbm, first.at[0])
    loads.add(parts_hbm.at[:, 0, 0], xs.at[0])

    def send(k, begin=0, stop=devices):
        where, count = pl.ds(begin, stop - begin), outs.shape[2]
        stores.start(outs.at[k, where], out_hbm.at[where, pl.ds(k * count, count)])

    for c in range(2):
        loads.begin(strips + 2 * c + 1)
        if c == 1:
            loads.take(strips)
        for k, (at, end) in enumerate(reversed(blocks)):
            if c == 0:
                loads.take(2 * k)
                loads.take(2 * k + 1)
                mask_factor(tiles_ref, left, at)
            g = gs[c, at // rows :].reshape(width - at, width)
            grad[c, at:end] = dot(left[at:, at:end], g, 0, 0).astype(BF)
    loads.begin(len(loads.all))
    loads.take(strips + 1)
    for at, _ in blocks:
        mask_factor(tiles_ref, right, at)
    loads.take(strips + 2)
    first_product(xs[1].reshape(width, width), right, first.at[1])
    mixed_product(left, first.at[1], outs.at[0], rows)
    send(0)
    loads.take(strips + 3)
    loads.take(strips + 4)

    core = place_ref[0] % 2
    side = width // tiles_ref.shape[0]
    per_tile = devices * side // width
    for at, end in blocks_of(width):
        sums = [None, None]
        for c in range(2):
            x, g = xs[c].reshape(width, width), gs[c].reshape(width, width)
            left_part = dot(g[at:end], first[c, :end], 1, 1)
            right_part = dot(grad[c, :, at:end], x[:, :end], 0, 0)
            for k, part in enumerate((left_part, right_part)):
                sums[k] = part if sums[k] is None else sums[k] + part
        for k in range(2):
            total[k, :, :, :, :, :end] = sums[k].reshape(total.shape[1:5] + (end,))
        for s in range(at // rows, end // rows):
            lower = s < devices // 2
            mirror = devices - 1 - s
            first_tile = 0 if lower else (mirror // per_tile) + 1
            for k in range(2):
                to = (s if lower else mirror) if k == 0 else (mirror if lower else s)
                for tile in range(s // per_tile + 1):
                    cols = slice(tile * LANES, (tile + 1) * LANES)
                    place = first_tile + tile
                    own = total[k, s - at // rows, :, core, :, cols]
                    keep[to, place] = own.reshape(SUB, LANES)
                    other = total[k, s - at // rows, :, 1 - core, :, cols]
                    give[to, place] = other.reshape(SUB, LANES).astype(BF)

    for c in range(2):
        for begin, stop in blocks:
            for at, end in blocks:
                part = dot(grad[c, begin:stop, at:], right[at:, at:end], 1, 0).astype(BF)
                lead_device = begin // rows
                put_tiles(outs.at[1 + c], lead_device, part, rows, at // LANES, width // LANES)
            send(1 + c, begin // rows, stop // rows)
    stores.wait()


def rest(place, tiles, left, right, parts, first, own):
    devices, _, _, rows, width = parts.shape
    halves = rows // SUB
    count = width // LANES * halves
    terms = tiles.shape[0] + 1
    smem = pl.BlockSpec(memory_space=pltpu.SMEM)
    whole = pl.BlockSpec(memory_space=pl.ANY)
    vmem = pl.BlockSpec(memory_space=pltpu.VMEM)
    square = pltpu.VMEM((width, width), BF)
    channels = pltpu.VMEM((2, devices, rows, width), BF)
    squares = pltpu.VMEM((2, width, width), BF)
    dims = (devices, terms, SUB, LANES)
    return pl.pallas_call(
        rest_kernel,
        in_specs=[smem, smem] + [whole] * 4,
        out_specs=(whole, vmem, vmem),
        out_shape=(
            pltpu.HBM((devices, 3 * count + terms, SUB, LANES), BF),
            pltpu.VMEM(dims, F32),
            pltpu.VMEM(dims, BF),
        ),
        scratch_shapes=[
            square,
            square,
            channels,
            channels,
            squares,
            squares,
            pltpu.VMEM((3, devices, count, SUB, LANES), BF),
            pltpu.VMEM((2, SIDE // rows, halves, 2, own, width), F32),
            pltpu.SemaphoreType.DMA((5 + 2 * width // SIDE,)),
            pltpu.SemaphoreType.DMA((1 + 2 * width // SIDE,)),
        ],
        compiler_params=params(56),
    )(place, tiles, in_hbm(left), in_hbm(right), in_hbm(parts), in_hbm(first))


def add_kernel(keep_ref, got_ref, parts_ref, out_ref, total, sem):
    total[...] = (keep_ref[...] + got_ref[...].astype(F32)).astype(BF)
    terms = total.shape[1]
    copy = pltpu.make_async_copy(
        total, out_ref.at[:, pl.ds(out_ref.shape[1] - terms, terms)], sem
    )
    copy.start()
    copy.wait()


def add(keep, got, parts):
    vmem = pl.BlockSpec(memory_space=pltpu.VMEM)
    whole = pl.BlockSpec(memory_space=pl.ANY)
    return pl.pallas_call(
        add_kernel,
        in_specs=[vmem, vmem, whole],
        out_specs=whole,
        out_shape=pltpu.HBM(parts.shape, BF),
        input_output_aliases={2: 0},
        scratch_shapes=[pltpu.VMEM(keep.shape, BF), pltpu.SemaphoreType.DMA],
        compiler_params=params(16),
    )(keep, got, in_hbm(parts))


def tie_kernel(parts_ref, after_ref, out_ref):
    pass


def tie(parts, after):
    whole = pl.BlockSpec(memory_space=pl.ANY)
    return pl.pallas_call(
        tie_kernel,
        in_specs=[whole, whole],
        out_specs=whole,
        out_shape=pltpu.HBM(parts.shape, BF),
        input_output_aliases={0: 0},
    )(in_hbm(parts), after)


def fold_kernel(parts_ref, out_ref, got, sem):
    _, terms, own, _ = out_ref.shape
    copy = pltpu.make_async_copy(
        parts_ref.at[:, pl.ds(parts_ref.shape[1] - terms, terms)], got, sem
    )
    copy.start()
    copy.wait()
    total = jnp.sum(got[...].astype(F32), 0).reshape(terms, 2, own, LANES)
    for k in range(4):
        out_ref[k] = total[:, k % 2]


def fold(parts, terms, own):
    return pl.pallas_call(
        fold_kernel,
        in_specs=[pl.BlockSpec(memory_space=pl.ANY)],
        out_specs=pl.BlockSpec(memory_space=pltpu.VMEM),
        out_shape=shape((4, terms, own, LANES), F32),
        scratch_shapes=[
            pltpu.VMEM((parts.shape[0], terms, SUB, LANES), BF),
            pltpu.SemaphoreType.DMA,
        ],
        compiler_params=params(16),
    )(in_hbm(parts))


def finish_kernel(devices, scale, place_ref, tiles_ref, got_ref, left_ref, right_ref, total):
    count = tiles_ref.shape[0]
    total[0] = got_ref[0] + got_ref[1]
    total[1] = got_ref[2] + got_ref[3]
    row = place_ref[1] // (devices // count)
    start = jnp.where(place_ref[1] < devices // 2, 0, count - row)
    for tile in range(count):
        lanes = slice(tile * LANES, (tile + 1) * LANES)
        factor = tiles_ref[row, tile].astype(F32) * scale
        at = jnp.minimum(start + tile, count)
        left_ref[:, lanes] = total[0, at] * factor
        right_ref[:, lanes] = total[1, at] * factor


def finish(place, tiles, got, devices, scale):
    _, terms, own, _ = got.shape
    smem = pl.BlockSpec(memory_space=pltpu.SMEM)
    vmem = pl.BlockSpec(memory_space=pltpu.VMEM)
    out = shape((own, (terms - 1) * LANES), F32)
    return pl.pallas_call(
        lambda *refs: finish_kernel(devices, scale, *refs),
        in_specs=[smem, smem, vmem],
        out_specs=(vmem, vmem),
        out_shape=(out, out),
        scratch_shapes=[pltpu.VMEM((2, terms, own, LANES), F32)],
        compiler_params=params(16),
    )(place, tiles, got)


def swap(x):
    return lax.all_to_all(x, "seq", split_axis=0, concat_axis=0, tiled=True)


def shards(inputs, gate_in, cotangent, right_factor, left_factor, mask_tiles):
    width = right_factor.shape[0]
    rows, channels = inputs.shape[1], inputs.shape[2]
    seq_count = lax.axis_size("seq")
    data_count = lax.axis_size("dp")
    own = width // (seq_count * data_count)
    place = jnp.stack((lax.axis_index("dp"), lax.axis_index("seq"))).astype(jnp.int32)

    parts, place = spread(place, inputs, cotangent, gate_in)
    parts = swap(parts)
    ahead, first = lead(mask_tiles, left_factor, right_factor, parts)
    ahead = swap(ahead)
    parts, keep, give = rest(
        place, mask_tiles, left_factor, right_factor, parts, first, own
    )
    got = lax.ppermute(give, "dp", [(d, d ^ 1) for d in range(data_count)])
    parts = swap(tie(add(keep, got, parts), ahead[0, 0]))
    sums = fold(parts, mask_tiles.shape[0] + 1, own)
    groups = [
        [at * data_count + d for at in (s, seq_count - 1 - s) for d in (core, core + 2)]
        for s in range(seq_count // 2)
        for core in range(2)
    ]
    got = lax.all_to_all(
        sums,
        ("seq", "dp"),
        split_axis=0,
        concat_axis=0,
        tiled=True,
        axis_index_groups=groups,
    )
    grad_input, grad_gate = gather(ahead, parts, cotangent, gate_in, sums)
    scale = 1.0 / math.sqrt(data_count * channels * width)
    grad_left, grad_right = finish(place, mask_tiles, got, seq_count, scale)
    return grad_input, grad_gate, grad_right, grad_left


def solution(mesh):
    placed = (
        P("dp", "seq", None, None),
        P("dp", "seq", None, None),
        P("dp", "seq", None, None),
        P(),
        P(),
        P(),
    )
    return jax.shard_map(
        shards,
        mesh=mesh,
        in_specs=placed,
        out_specs=(
            P("dp", "seq", None, None),
            P("dp", "seq", None, None),
            P(("seq", "dp"), None),
            P(("seq", "dp"), None),
        ),
        check_vma=False,
    )
```

```python
import math

import jax
import jax.numpy as jnp
from jax import lax
from jax.experimental import pallas as pl
from jax.experimental.pallas import tpu as pltpu
from jax.sharding import PartitionSpec as P

BF = jnp.bfloat16
F32 = jnp.float32
MIB = 1024 * 1024
LANES = 128
SUB = 16
SIDE = 256


def params(mib):
    return pltpu.CompilerParams(vmem_limit_bytes=mib * MIB)


def shape(dims, dtype):
    return jax.ShapeDtypeStruct(dims, dtype)


def in_hbm(x):
    return pltpu.with_memory_space_constraint(x, pltpu.HBM)


def in_vmem(x):
    return pltpu.with_memory_space_constraint(x, pltpu.VMEM)


def dot(a, b, on_a, on_b):
    return lax.dot_general(a, b, (((on_a,), (on_b,)), ((), ())), preferred_element_type=F32)


class Copies:
    def __init__(self, sems):
        self.sems, self.all, self.begun = sems, [], 0

    def add(self, src, dst):
        self.all.append(pltpu.make_async_copy(src, dst, self.sems.at[len(self.all)]))
        return len(self.all) - 1

    def begin(self, count):
        for copy in self.all[self.begun : count]:
            copy.start()
        self.begun = max(self.begun, min(count, len(self.all)))

    def start(self, src, dst):
        self.add(src, dst)
        self.begin(len(self.all))

    def take(self, index, ahead=0):
        self.begin(index + 1 + ahead)
        self.all[index].wait()

    def wait(self):
        for copy in self.all:
            copy.wait()


def put_tiles(ref, lead, part, rows, first_tile, tiles):
    devices, halves = part.shape[0] // rows, rows // SUB
    for tile in range(part.shape[1] // LANES):
        piece = part[:, tile * LANES : (tile + 1) * LANES].reshape(devices, halves, SUB, LANES)
        for half in range(halves):
            at = half * tiles + first_tile + tile
            ref[lead : lead + devices, at] = piece[:, half]


def turning():
    size = SUB * SUB
    row = lax.broadcasted_iota(jnp.int32, (size, size), 0)
    col = lax.broadcasted_iota(jnp.int32, (size, size), 1)
    return jnp.where(col == row % SUB * SUB + row // SUB, 1.0, 0.0).astype(BF)


def chunks_of(rows, channels):
    for group in range(channels // SUB):
        devices = pl.ds(group * SUB // 2, SUB // 2)
        for half in range(rows // SUB):
            yield half, pl.ds(half * SUB, SUB), pl.ds(group * SUB, SUB), devices


def spread_kernel(
    place_ref, x_hbm, cot_hbm, gate_hbm, out, place_out_ref,
    x, cot, gate, in_sems,
):
    for k in range(place_ref.shape[0]):
        place_out_ref[k] = place_ref[k]
    _, rows, channels, width = x.shape
    size, dims = SUB * SUB, (SUB // 2, 2, SUB, width)
    loads = Copies(in_sems)
    chunks, turned = list(chunks_of(rows, channels)), turning()
    for _, at, group, _ in chunks:
        loads.add(x_hbm.at[0, at, group], x.at[0, at, group])
    for _, at, group, _ in chunks:
        for src, dst in ((cot_hbm, cot), (gate_hbm, gate)):
            loads.add(src.at[0, at, group], dst.at[0, at, group])
    count = len(chunks)
    loads.begin(count + 4)
    for k, (_, at, group, devices) in enumerate(chunks):
        loads.take(k)
        loads.begin(count + 6 + 2 * k)
        part = dot(turned, x[0, at, group].reshape(size, width), 1, 0)
        out[devices, :, 0, at] = part.astype(BF).reshape(dims)
    loads.begin(len(loads.all))
    for k, (_, at, group, devices) in enumerate(chunks):
        for copy in range(2):
            loads.take(count + 2 * k + copy)
        tanh = jnp.tanh(gate[0, at, group].astype(F32) * 0.5)
        grad = (cot[0, at, group].astype(F32) * (0.5 + 0.5 * tanh)).astype(BF)
        part = dot(turned, grad.reshape(size, width), 1, 0)
        out[devices, :, 1, at] = part.astype(BF).reshape(dims)


def spread(place, x, cot, gate):
    _, rows, channels, width = x.shape
    smem = pl.BlockSpec(memory_space=pltpu.SMEM)
    whole = pl.BlockSpec(memory_space=pl.ANY)
    dims = (channels // 2, 2, 2, rows, width)
    count = rows * channels // (SUB * SUB)
    return pl.pallas_call(
        spread_kernel,
        in_specs=[smem] + [whole] * 3,
        out_specs=(pl.BlockSpec(memory_space=pltpu.VMEM), smem),
        out_shape=(pltpu.VMEM(dims, BF), shape(place.shape, place.dtype)),
        scratch_shapes=[pltpu.VMEM(x.shape, BF)] * 3 + [pltpu.SemaphoreType.DMA((3 * count,))],
        compiler_params=params(48),
    )(place, in_hbm(x), in_hbm(cot), in_hbm(gate))


def gather_kernel(
    lead_hbm, in_hbm_ref, cot_hbm, gate_hbm, after_ref, back_hbm, grad_hbm,
    ahead, parts, cot, gate, back, grad, in_sems, out_sems,
):
    _, rows, channels, width = cot.shape
    size, dims = SUB * SUB, (SUB, SUB, width)
    tiles, halves = width // LANES, rows // SUB
    loads, stores = Copies(in_sems), Copies(out_sems)
    chunks, turned = list(chunks_of(rows, channels)), turning()

    def tiles_at(half, k):
        return pl.ds((k * halves + half) * tiles, tiles)

    for half, at, group, devices in chunks:
        where = (devices, tiles_at(half, 0))
        loads.add(lead_hbm.at[where], ahead.at[where])
        for k in range(3):
            where = (devices, tiles_at(half, k))
            loads.add(in_hbm_ref.at[where], parts.at[where])
        for src, dst in ((cot_hbm, cot), (gate_hbm, gate)):
            loads.add(src.at[0, at, group], dst.at[0, at, group])

    def rows_of(both, half, devices):
        columns = []
        for tile in range(tiles):
            pair = [ref[devices, (k * halves + half) * tiles + tile] for ref, k in both]
            columns.append(jnp.stack(pair, 1).reshape(size, LANES))
        return dot(turned, jnp.concatenate(columns, 1), 1, 0)

    loads.begin(len(loads.all))
    for k, (half, at, group, devices) in enumerate(chunks):
        for copy in range(6):
            loads.take(6 * k + copy)
        part = rows_of(((parts, 1), (parts, 2)), half, devices)
        back[0, at, group] = part.astype(BF).reshape(dims)
        stores.start(back.at[0, at, group], back_hbm.at[0, at, group])
        mixed = rows_of(((ahead, 0), (parts, 0)), half, devices).reshape(dims)
        tanh = jnp.tanh(gate[0, at, group].astype(F32) * 0.5)
        slope = 0.25 * (1.0 - tanh) * (1.0 + tanh)
        grad[0, at, group] = (cot[0, at, group].astype(F32) * mixed * slope).astype(BF)
        stores.start(grad.at[0, at, group], grad_hbm.at[0, at, group])
    stores.wait()


def gather(ahead, parts, cot, gate, after):
    _, rows, channels, width = cot.shape
    whole = pl.BlockSpec(memory_space=pl.ANY)
    devices, blocks = ahead.shape[:2]
    count = rows * channels // (SUB * SUB)
    natural = pltpu.VMEM(cot.shape, BF)
    return pl.pallas_call(
        gather_kernel,
        in_specs=[whole] * 5,
        out_specs=(whole, whole),
        out_shape=(pltpu.HBM(cot.shape, BF), pltpu.HBM(cot.shape, BF)),
        scratch_shapes=[
            pltpu.VMEM(ahead.shape, BF),
            pltpu.VMEM((devices, 3 * blocks, SUB, LANES), BF),
            natural,
            natural,
            natural,
            natural,
            pltpu.SemaphoreType.DMA((6 * count,)),
            pltpu.SemaphoreType.DMA((2 * count,)),
        ],
        compiler_params=params(48),
    )(ahead, in_hbm(parts), cot, gate, after)


def mask_factor(tiles_ref, ref, begin):
    count = tiles_ref.shape[0]
    side = ref.shape[0] // count
    for a in range(begin // side, (begin + SIDE) // side):
        for b in range((begin + SIDE) // side):
            where = (slice(a * side, (a + 1) * side), slice(b * side, (b + 1) * side))
            if b > a:
                ref[where] = jnp.zeros((side, side), BF)
            else:
                keep = jnp.full((side, side), tiles_ref[a, b].astype(F32)).astype(BF)
                ref[where] = ref[where] * keep


def blocks_of(width):
    return [(at, at + SIDE) for at in range(0, width, SIDE)]


def first_product(x, right, first):
    for at, end in blocks_of(x.shape[0]):
        first[:, at:end] = dot(x[:, :end], right[at:end, :end], 1, 1).astype(BF)


def mixed_product(left, first, mixed, rows):
    for at, end in blocks_of(left.shape[0]):
        part = dot(left[at:end, :end], first[:end], 1, 0).astype(BF)
        put_tiles(mixed, at // rows, part, rows, 0, part.shape[1] // LANES)


def lead_kernel(
    tiles_ref, left_hbm, right_hbm, parts_hbm, out_hbm, first_hbm,
    left, right, x, first, mixed, in_sems, out_sems,
):
    width, rows = left.shape[0], x.shape[1]
    blocks = blocks_of(width)
    loads, stores = Copies(in_sems), Copies(out_sems)

    count = len(blocks)

    def strip_of(src, dst, at, end):
        strip = (pl.ds(at, SIDE), pl.ds(0, end))
        loads.add(src.at[strip], dst.at[strip])

    for at, end in blocks:
        strip_of(right_hbm, right, at, end)
    for at, end in blocks:
        devices = pl.ds(at // rows, SIDE // rows)
        loads.add(parts_hbm.at[devices, 0, 0], x.at[devices])
    for at, end in blocks:
        strip_of(left_hbm, left, at, end)
    loads.begin(2 * count)
    for k, (at, _) in enumerate(blocks):
        loads.take(k)
        mask_factor(tiles_ref, right, at)
    loads.begin(3 * count)
    for k, (begin, stop) in enumerate(blocks):
        loads.take(count + k)
        strip = x[begin // rows : stop // rows].reshape(SIDE, width)
        for at, end in blocks:
            part = dot(strip[:, :end], right[at:end, :end], 1, 1)
            first[begin:stop, at:end] = part.astype(BF)
        stores.start(first.at[pl.ds(begin, SIDE)], first_hbm.at[pl.ds(begin, SIDE)])
    for k, (at, end) in enumerate(blocks):
        loads.take(2 * count + k)
        mask_factor(tiles_ref, left, at)
        part = dot(left[at:end, :end], first[:end], 1, 0).astype(BF)
        put_tiles(mixed, at // rows, part, rows, 0, width // LANES)
        devices = pl.ds(at // rows, SIDE // rows)
        stores.start(mixed.at[devices], out_hbm.at[devices])
    stores.wait()


def lead(tiles, left, right, parts):
    devices, _, _, rows, width = parts.shape
    whole = pl.BlockSpec(memory_space=pl.ANY)
    square = pltpu.VMEM((width, width), BF)
    dims = (devices, rows * width // (SUB * LANES), SUB, LANES)
    return pl.pallas_call(
        lead_kernel,
        in_specs=[pl.BlockSpec(memory_space=pltpu.SMEM), whole, whole, whole],
        out_specs=(whole, whole),
        out_shape=(pltpu.HBM(dims, BF), pltpu.HBM((width, width), BF)),
        scratch_shapes=[
            square,
            square,
            pltpu.VMEM((devices, rows, width), BF),
            square,
            pltpu.VMEM(dims, BF),
            pltpu.SemaphoreType.DMA((3 * width // SIDE,)),
            pltpu.SemaphoreType.DMA((2 * width // SIDE,)),
        ],
        compiler_params=params(32),
    )(tiles, left, right, in_hbm(parts))


def rest_kernel(
    place_ref, tiles_ref, left_hbm, right_hbm, parts_hbm, first_hbm,
    out_hbm, keep, give,
    left, right, xs, gs, first, grad, outs, total, in_sems, out_sems,
):
    width, rows = left.shape[0], xs.shape[2]
    devices = width // rows
    loads, stores = Copies(in_sems), Copies(out_sems)
    blocks = blocks_of(width)
    for at, end in reversed(blocks):
        strip = (pl.ds(at, SIDE), pl.ds(0, end))
        loads.add(left_hbm.at[strip], left.at[strip])
        devices_at = pl.ds(at // rows, SIDE // rows)
        loads.add(parts_hbm.at[devices_at, 0, 1], gs.at[0, devices_at])
    strips = len(loads.all)
    loads.add(parts_hbm.at[:, 1, 1], gs.at[1])
    loads.add(right_hbm, right)
    loads.add(parts_hbm.at[:, 1, 0], xs.at[1])
    loads.add(first_hbm, first.at[0])
    loads.add(parts_hbm.at[:, 0, 0], xs.at[0])

    def send(k, begin=0, stop=devices):
        where, count = pl.ds(begin, stop - begin), outs.shape[2]
        stores.start(outs.at[k, where], out_hbm.at[where, pl.ds(k * count, count)])

    for c in range(2):
        loads.begin(strips + 2 * c + 1)
        if c == 1:
            loads.take(strips)
        for k, (at, end) in enumerate(reversed(blocks)):
            if c == 0:
                loads.take(2 * k)
                loads.take(2 * k + 1)
                mask_factor(tiles_ref, left, at)
            g = gs[c, at // rows :].reshape(width - at, width)
            grad[c, at:end] = dot(left[at:, at:end], g, 0, 0).astype(BF)
    loads.begin(len(loads.all))
    loads.take(strips + 1)
    for at, _ in blocks:
        mask_factor(tiles_ref, right, at)
    loads.take(strips + 2)
    first_product(xs[1].reshape(width, width), right, first.at[1])
    mixed_product(left, first.at[1], outs.at[0], rows)
    send(0)
    loads.take(strips + 3)
    loads.take(strips + 4)

    core = place_ref[0] % 2
    side = width // tiles_ref.shape[0]
    per_tile = devices * side // width
    for at, end in blocks_of(width):
        sums = [None, None]
        for c in range(2):
            x, g = xs[c].reshape(width, width), gs[c].reshape(width, width)
            left_part = dot(g[at:end], first[c, :end], 1, 1)
            right_part = dot(grad[c, :, at:end], x[:, :end], 0, 0)
            for k, part in enumerate((left_part, right_part)):
                sums[k] = part if sums[k] is None else sums[k] + part
        for k in range(2):
            total[k, :, :, :, :, :end] = sums[k].reshape(total.shape[1:5] + (end,))
        for s in range(at // rows, end // rows):
            lower = s < devices // 2
            mirror = devices - 1 - s
            first_tile = 0 if lower else (mirror // per_tile) + 1
            for k in range(2):
                to = (s if lower else mirror) if k == 0 else (mirror if lower else s)
                for tile in range(s // per_tile + 1):
                    cols = slice(tile * LANES, (tile + 1) * LANES)
                    place = first_tile + tile
                    own = total[k, s - at // rows, :, core, :, cols]
                    keep[to, place] = own.reshape(SUB, LANES)
                    other = total[k, s - at // rows, :, 1 - core, :, cols]
                    give[to, place] = other.reshape(SUB, LANES).astype(BF)

    for c in range(2):
        for begin, stop in blocks:
            for at, end in blocks:
                part = dot(grad[c, begin:stop, at:], right[at:, at:end], 1, 0).astype(BF)
                lead_device = begin // rows
                put_tiles(outs.at[1 + c], lead_device, part, rows, at // LANES, width // LANES)
            send(1 + c, begin // rows, stop // rows)
    stores.wait()


def rest(place, tiles, left, right, parts, first, own):
    devices, _, _, rows, width = parts.shape
    halves = rows // SUB
    count = width // LANES * halves
    terms = tiles.shape[0] + 1
    smem = pl.BlockSpec(memory_space=pltpu.SMEM)
    whole = pl.BlockSpec(memory_space=pl.ANY)
    vmem = pl.BlockSpec(memory_space=pltpu.VMEM)
    square = pltpu.VMEM((width, width), BF)
    channels = pltpu.VMEM((2, devices, rows, width), BF)
    squares = pltpu.VMEM((2, width, width), BF)
    dims = (devices, terms, SUB, LANES)
    return pl.pallas_call(
        rest_kernel,
        in_specs=[smem, smem] + [whole] * 4,
        out_specs=(whole, vmem, vmem),
        out_shape=(
            pltpu.HBM((devices, 3 * count + terms, SUB, LANES), BF),
            pltpu.VMEM(dims, F32),
            pltpu.VMEM(dims, BF),
        ),
        scratch_shapes=[
            square,
            square,
            channels,
            channels,
            squares,
            squares,
            pltpu.VMEM((3, devices, count, SUB, LANES), BF),
            pltpu.VMEM((2, SIDE // rows, halves, 2, own, width), F32),
            pltpu.SemaphoreType.DMA((5 + 2 * width // SIDE,)),
            pltpu.SemaphoreType.DMA((1 + 2 * width // SIDE,)),
        ],
        compiler_params=params(56),
    )(place, tiles, in_hbm(left), in_hbm(right), in_hbm(parts), in_hbm(first))


def add_kernel(keep_ref, got_ref, parts_ref, out_ref, total, sem):
    total[...] = (keep_ref[...] + got_ref[...].astype(F32)).astype(BF)
    terms = total.shape[1]
    copy = pltpu.make_async_copy(
        total, out_ref.at[:, pl.ds(out_ref.shape[1] - terms, terms)], sem
    )
    copy.start()
    copy.wait()


def add(keep, got, parts):
    vmem = pl.BlockSpec(memory_space=pltpu.VMEM)
    whole = pl.BlockSpec(memory_space=pl.ANY)
    return pl.pallas_call(
        add_kernel,
        in_specs=[vmem, vmem, whole],
        out_specs=whole,
        out_shape=pltpu.HBM(parts.shape, BF),
        input_output_aliases={2: 0},
        scratch_shapes=[pltpu.VMEM(keep.shape, BF), pltpu.SemaphoreType.DMA],
        compiler_params=params(16),
    )(keep, got, in_hbm(parts))


def tie_kernel(parts_ref, after_ref, out_ref):
    pass


def tie(parts, after):
    whole = pl.BlockSpec(memory_space=pl.ANY)
    return pl.pallas_call(
        tie_kernel,
        in_specs=[whole, pl.BlockSpec(memory_space=pltpu.VMEM)],
        out_specs=whole,
        out_shape=pltpu.HBM(parts.shape, BF),
        input_output_aliases={0: 0},
    )(in_hbm(parts), in_vmem(after))


def fold_kernel(parts_ref, out_ref, got, sem):
    _, terms, own, _ = out_ref.shape
    copy = pltpu.make_async_copy(
        parts_ref.at[:, pl.ds(parts_ref.shape[1] - terms, terms)], got, sem
    )
    copy.start()
    copy.wait()
    total = jnp.sum(got[...].astype(F32), 0).reshape(terms, 2, own, LANES)
    for k in range(4):
        out_ref[k] = total[:, k % 2]


def fold(parts, terms, own):
    return pl.pallas_call(
        fold_kernel,
        in_specs=[pl.BlockSpec(memory_space=pl.ANY)],
        out_specs=pl.BlockSpec(memory_space=pltpu.VMEM),
        out_shape=shape((4, terms, own, LANES), F32),
        scratch_shapes=[
            pltpu.VMEM((parts.shape[0], terms, SUB, LANES), BF),
            pltpu.SemaphoreType.DMA,
        ],
        compiler_params=params(16),
    )(in_hbm(parts))


def finish_kernel(devices, scale, place_ref, tiles_ref, got_ref, left_ref, right_ref, total):
    count = tiles_ref.shape[0]
    total[0] = got_ref[0] + got_ref[1]
    total[1] = got_ref[2] + got_ref[3]
    row = place_ref[1] // (devices // count)
    start = jnp.where(place_ref[1] < devices // 2, 0, count - row)
    for tile in range(count):
        lanes = slice(tile * LANES, (tile + 1) * LANES)
        factor = tiles_ref[row, tile].astype(F32) * scale
        at = jnp.minimum(start + tile, count)
        left_ref[:, lanes] = total[0, at] * factor
        right_ref[:, lanes] = total[1, at] * factor


def finish(place, tiles, got, devices, scale):
    _, terms, own, _ = got.shape
    smem = pl.BlockSpec(memory_space=pltpu.SMEM)
    vmem = pl.BlockSpec(memory_space=pltpu.VMEM)
    out = shape((own, (terms - 1) * LANES), F32)
    return pl.pallas_call(
        lambda *refs: finish_kernel(devices, scale, *refs),
        in_specs=[smem, smem, vmem],
        out_specs=(vmem, vmem),
        out_shape=(out, out),
        scratch_shapes=[pltpu.VMEM((2, terms, own, LANES), F32)],
        compiler_params=params(16),
    )(place, tiles, got)


def swap(x):
    return lax.all_to_all(x, "seq", split_axis=0, concat_axis=0, tiled=True)


def shards(inputs, gate_in, cotangent, right_factor, left_factor, mask_tiles):
    width = right_factor.shape[0]
    rows, channels = inputs.shape[1], inputs.shape[2]
    seq_count = lax.axis_size("seq")
    data_count = lax.axis_size("dp")
    own = width // (seq_count * data_count)
    place = jnp.stack((lax.axis_index("dp"), lax.axis_index("seq"))).astype(jnp.int32)

    parts, place = spread(place, inputs, cotangent, gate_in)
    parts = swap(parts)
    ahead, first = lead(mask_tiles, left_factor, right_factor, parts)
    ahead = swap(ahead)
    parts, keep, give = rest(
        place, mask_tiles, left_factor, right_factor, parts, first, own
    )
    got = lax.ppermute(give, "dp", [(d, d ^ 1) for d in range(data_count)])
    parts = swap(tie(add(keep, got, parts), ahead))
    sums = fold(parts, mask_tiles.shape[0] + 1, own)
    groups = [
        [at * data_count + d for at in (s, seq_count - 1 - s) for d in (core, core + 2)]
        for s in range(seq_count // 2)
        for core in range(2)
    ]
    got = lax.all_to_all(
        sums,
        ("seq", "dp"),
        split_axis=0,
        concat_axis=0,
        tiled=True,
        axis_index_groups=groups,
    )
    grad_input, grad_gate = gather(ahead, parts, cotangent, gate_in, sums)
    scale = 1.0 / math.sqrt(data_count * channels * width)
    grad_left, grad_right = finish(place, mask_tiles, got, seq_count, scale)
    return grad_input, grad_gate, grad_right, grad_left


def solution(mesh):
    placed = (
        P("dp", "seq", None, None),
        P("dp", "seq", None, None),
        P("dp", "seq", None, None),
        P(),
        P(),
        P(),
    )
    return jax.shard_map(
        shards,
        mesh=mesh,
        in_specs=placed,
        out_specs=(
            P("dp", "seq", None, None),
            P("dp", "seq", None, None),
            P(("seq", "dp"), None),
            P(("seq", "dp"), None),
        ),
        check_vma=False,
    )
```
